512 devices in a mesh: dp: 64 (over z, y_lo, core), mp: 8 (over x, y_hi).
Axes of the slice: x: 4, y: 4 (y_hi: 2, y_lo: 2; y = y_hi * 2 + y_lo), z: 16, core: 2. Of those that a mesh axis runs over, the one named last changes fastest.
Arguments:
- attn_out: bfloat16 [16384, 7168], P('dp', 'mp'), may hold values from -6 to 6
- out_grad: bfloat16 [16384, 7168], P('dp', 'mp'), may hold values from -6 to 6
- projection: bfloat16 [7168, 256], P('dp'), may hold values from -0.0625 to 0.0625
- momentum: float32 [7168, 256], P('mp'), may hold values from -6 to 6
- weight: bfloat16 [7168, 7168], P('mp', 'dp'), may hold values from -6 to 6
Outputs:
- new_momentum: float32 [7168, 256], P('mp')
- new_weight: bfloat16 [7168, 7168], P('mp', 'dp')
The draws below stay inside these ranges and needn't reach their ends.
All inputs are finite; a program needn't handle non-finite values.
Results may differ from the reference program's by a relative error of at most 0.0075.
Values may be sent and summed in bfloat16 or wider, within the bound.
A program may use at most 128 MiB of HBM per device.

```python
import math
import jax
import jax.numpy as jnp
from jax import lax

D = 7168
R = 256
INNER = 7168
TOKENS = 16384


def steps_of(stream_key, shape, cuts, least, high):
    def one(position, shards_of):
        draws = jax.random.uniform(jax.random.fold_in(jax.random.fold_in(stream_key, 6), position), (shards_of,), jnp.float32, least / len(cuts), high / len(cuts))
        return jnp.repeat(jnp.exp(draws), shape[position] // shards_of).reshape((-1,) + (1,) * (len(shape) - position - 1))

    loudness = one(*cuts[0])
    for cut in cuts[1:]:
        loudness = loudness * one(*cut)
    return loudness


def centred(own_key, dims, spread, reach, shards=(), kind=jnp.bfloat16):
    array = jax.random.normal(own_key, dims, jnp.float32) * spread
    if len(shards) > 0:
        array = steps_of(own_key, dims, shards, -0.22, 0.18) * array
    return jnp.clip(array, min=-reach, max=reach).astype(kind)


def setup_inputs(seed: int = 0) -> dict:
    keys = jax.random.split(jax.random.key(seed), 6)
    attn_out = centred(keys[0], (TOKENS, INNER), 1.0, 6.0, ((0, 64), (1, 8)))
    out_grad = centred(keys[1], (TOKENS, D), 1.0, 6.0, ((0, 64), (1, 8)))
    projection = centred(keys[2], (D, R), D ** -0.5, 0.0625, ((0, 64),))
    momentum = centred(keys[3], (INNER, R), 1.0, 6.0, ((0, 8),), jnp.float32)
    weight = centred(keys[4], (INNER, D), 1.0, 6.0, ((0, 8), (1, 64)))
    return {"attn_out": attn_out, "out_grad": out_grad, "projection": projection, "momentum": momentum, "weight": weight}


def reference(attn_out, out_grad, projection, momentum, weight):
    factor = 1.0 / math.sqrt(TOKENS)
    reduced = jnp.dot(out_grad, projection, preferred_element_type=jnp.float32)
    compressed = jnp.dot(attn_out.astype(jnp.float32).T, reduced, precision=lax.Precision.HIGHEST) * factor
    new_momentum = 0.9 * momentum + compressed
    update = jnp.dot(new_momentum, projection.astype(jnp.float32).T, precision=lax.Precision.HIGHEST)
    new_weight = (weight.astype(jnp.float32) - 2.0 * update).astype(jnp.bfloat16)
    return (new_momentum, new_weight)
```

```python
import math

import jax
import jax.numpy as jnp
from jax import lax
from jax.sharding import PartitionSpec as P


def shards(attn_out, out_grad, projection, momentum, weight):
    tok_rows = attn_out.shape[0]
    cols = out_grad.shape[1]
    factor = 1.0 / math.sqrt(tok_rows * lax.axis_size("dp"))
    whole = lax.all_gather(projection, "dp", axis=0, tiled=True)
    mine = lax.dynamic_slice_in_dim(whole, lax.axis_index("mp") * cols, cols, axis=0)
    part = jnp.dot(out_grad, mine, preferred_element_type=jnp.float32)
    reduced = lax.psum(part, "mp").astype(jnp.bfloat16)
    compressed_local = lax.dot_general(
        attn_out, reduced, (((0,), (0,)), ((), ())), preferred_element_type=jnp.float32
    )
    compressed = lax.psum(compressed_local * factor, "dp")
    new_momentum = 0.9 * momentum + compressed
    update = lax.dot_general(
        new_momentum.astype(jnp.bfloat16),
        projection,
        (((1,), (1,)), ((), ())),
        preferred_element_type=jnp.float32,
    )
    new_weight = (weight.astype(jnp.float32) - 2.0 * update).astype(jnp.bfloat16)
    return (new_momentum, new_weight)


def solution(mesh):
    return jax.shard_map(
        shards,
        mesh=mesh,
        in_specs=(P("dp", "mp"), P("dp", "mp"), P("dp", None), P("mp", None), P("mp", "dp")),
        out_specs=(P("mp", None), P("mp", "dp")),
        check_vma=False,
    )
```

```python
import functools
import math

import jax
import jax.numpy as jnp
from jax import lax
from jax.experimental import pallas as pl
from jax.experimental.pallas import tpu as pltpu
from jax.sharding import PartitionSpec as P

MESH = pl.DeviceIdType.MESH
BF16 = jnp.bfloat16
F32 = jnp.float32

NZ, NM = 16, 8
BLK = 112
SL = 16
SLICES = 7
TOK, COLS, RANK = 256, 896, 256
HALF = RANK // 2
PIECE = TOK // NM
CHUNK = COLS // 8
NEAR = (0, 1, -1, -2)
FAR_FIRST = (8, 7, 9, 6, 10, 5, 11, 4, 12, 3, 13, 2, 14, 1, 15)
NEAR_FIRST = (0, 1, 7, 2, 6, 3, 5, 4)


def kernel(
    factor,
    a_hbm, g_hbm, p_hbm, m_hbm, w_hbm,
    c_out, w_out,
    a, at, g, p, mom, w,
    pz, p2, pfull, part, rs, red,
    cown, csend, crecv, sb, rs2, far, cres,
    in_sem,
    p1s, p1r, p2s, p2r, p3s, p3r,
    r1s, r1r, r2s, r2r,
    d1s, d1r, d2s, d2r, d3s, d3r, d4s, d4r, d5s, d5r,
):
    dp, m = lax.axis_index("dp"), lax.axis_index("mp")
    z, yl, core = dp // 4, (dp // 2) % 2, dp % 2
    sign = 1 - 2 * core

    def dev(z_, yl_, core_, m_):
        return ((z_ * 2 + yl_) * 2 + core_, m_)

    sibling = dev(z, yl, 1 - core, m)

    def remote(src, dst, ssem, rsem, to):
        return pltpu.make_async_remote_copy(
            src_ref=src, dst_ref=dst, send_sem=ssem, recv_sem=rsem, device_id=to, device_id_type=MESH
        )

    def arrived(dst, rsem):
        remote(dst, dst, rsem, rsem, sibling).wait_recv()

    sent = []

    def send(src, dst, ssem, rsem, to):
        copy = remote(src, dst, ssem, rsem, to)
        copy.start()
        return copy

    loads = [
        pltpu.make_async_copy(src, dst, in_sem.at[i])
        for i, (src, dst) in enumerate(
            ((p_hbm, p), (a_hbm, a), (g_hbm, g), (m_hbm, mom), (w_hbm, w))
        )
    ]
    for load in loads:
        load.start()

    barrier = pltpu.get_barrier_semaphore()

    def greet(to):
        pl.semaphore_signal(barrier, inc=1, device_id=to, device_id_type=MESH)

    for k in FAR_FIRST:
        greet(dev((z + k) % NZ, yl, core, m))
    for k in range(1, NM):
        greet(dev(z, yl, core, (m + k) % NM))
    for k in range(NM):
        greet(dev(z, 1 - yl, core, (m + k) % NM))
    for k in (2, 14, 1, 15):
        greet(dev((z + k) % NZ, 1 - yl, core, m))
    greet(sibling)

    loads[0].wait()
    loads[1].wait()
    for k in range(COLS // 128):
        at[128 * k : 128 * (k + 1)] = a[:, 128 * k : 128 * (k + 1)].T

    pl.semaphore_wait(barrier, 15 + 7 + 8 + 4 + 1)

    @pl.when(m < SLICES)
    def _():
        rows = pl.ds(pl.multiple_of(jnp.minimum(m, SLICES - 1) * SL, SL), SL)
        pz[z] = p[rows]
        copies = [
            send(p.at[rows], pz.at[z], p1s.at[k], p1r.at[z], dev((z + k) % NZ, yl, core, m))
            for k in FAR_FIRST
        ]
        slot = jnp.minimum(m, SLICES - 1)
        for q in NEAR_FIRST:
            mt = (z // 2 + q) % NM
            for s in range(2):
                zs = 2 * mt + s
                if q == 0:
                    @pl.when(zs != z)
                    def _():
                        arrived(pz.at[zs], p1r.at[zs])
                else:
                    arrived(pz.at[zs], p1r.at[zs])
            src = pz.at[pl.ds(2 * mt, 2)]
            copies.append(
                send(src, p2.at[core, yl, slot], p2s.at[q], p2r.at[yl, slot], dev(z, 1 - yl, core, mt))
            )

            @pl.when(mt != m)
            def _():
                send(src, p2.at[core, yl, slot], p2s.at[NM + q], p2r.at[yl, slot], dev(z, yl, core, mt))

            @pl.when(mt == m)
            def _():
                p2[core, yl, slot] = pz[pl.ds(2 * mt, 2)]

        for copy in copies:
            copy.wait_send()
        for q in NEAR_FIRST:
            mt = (z // 2 + q) % NM

            @pl.when(mt != m)
            def _():
                remote(pz.at[pl.ds(2 * mt, 2)], p2.at[core, yl, slot], p2s.at[NM + q], p2r.at[yl, slot], sibling).wait_send()

    for ms in range(SLICES):
        for ys in range(2):
            @pl.when((ms != m) | (ys != yl))
            def _():
                arrived(p2.at[core, ys, ms], p2r.at[ys, ms])

            sent.append(send(p2.at[core, ys, ms], p2.at[core, ys, ms], p3s.at[ys, ms], p3r.at[ys, ms], sibling))
    for ms in range(SLICES):
        for ys in range(2):
            arrived(p2.at[1 - core, ys, ms], p3r.at[ys, ms])
    for c in range(2):
        for ys in range(2):
            for ms in range(SLICES):
                for s in range(2):
                    at_row = BLK * (4 * s + 2 * ys + c) + SL * ms
                    pfull[at_row : at_row + SL] = p2[c, ys, ms, s]

    loads[2].wait()
    part[...] = jnp.dot(g[...], pfull[...], preferred_element_type=F32).astype(BF16)

    def piece(i):
        return pl.ds(pl.multiple_of(i * PIECE, PIECE), PIECE)

    for k in range(1, NM):
        mt = (m + k) % NM
        sent.append(send(part.at[piece(mt)], rs.at[m], r1s.at[k], r1r.at[m], dev(z, yl, core, mt)))
    rs[m] = part[piece(m)]
    for k in range(1, NM):
        arrived(rs.at[(m + k) % NM], r1r.at[(m + k) % NM])
    total = rs[0].astype(F32)
    for i in range(1, NM):
        total += rs[i].astype(F32)
    red[piece(m)] = total.astype(BF16)
    for k in range(1, NM):
        mt = (m + k) % NM
        sent.append(send(red.at[piece(m)], red.at[piece(m)], r2s.at[k], r2r.at[m], dev(z, yl, core, mt)))
    for k in range(1, NM):
        mt = (m + k) % NM
        arrived(red.at[piece(mt)], r2r.at[mt])

    for k in range(COLS // 128):
        rows = slice(128 * k, 128 * (k + 1))
        tile = jnp.dot(at[rows], red[...], preferred_element_type=F32)
        low, high = tile[:, :HALF], tile[:, HALF:]
        cown[rows] = jnp.where(core == 0, low, high)
        csend[rows] = jnp.where(core == 0, high, low).astype(BF16)
    sent.append(send(csend, crecv, d1s, d1r, sibling))
    arrived(crecv, d1r)
    sb[...] = (cown[...] + crecv[...].astype(F32)).astype(BF16)

    def chunk(z_, yl_):
        return pl.ds(pl.multiple_of((2 * (z_ % 4) + yl_) * CHUNK, SL), CHUNK)

    for i in (3, 1, 2, 0):
        zo = (z + sign * NEAR[i] + NZ) % NZ
        for other in (1, 0):
            if i == 0 and other == 0:
                continue
            yo = (yl + other) % 2
            sent.append(
                send(sb.at[chunk(zo, yo)], rs2.at[i, yl], d2s.at[i, other], d2r.at[i, yl], dev(zo, yo, core, m))
            )
    rs2[0, yl] = sb[chunk(z, yl)]
    arrived(rs2.at[0, 1 - yl], d2r.at[0, 1 - yl])
    for i in (1, 2, 3):
        for y in range(2):
            arrived(rs2.at[i, y], d2r.at[i, y])
    total = rs2[0, 0].astype(F32) + rs2[0, 1].astype(F32)
    for i in (1, 2, 3):
        total += rs2[i, 0].astype(F32) + rs2[i, 1].astype(F32)
    zh = z // 4
    far[zh] = total.astype(BF16)
    for k in (2, 1, 3):
        sent.append(send(far.at[zh], far.at[zh], d3s.at[k], d3r.at[zh], dev((z + 4 * k) % NZ, yl, core, m)))
    for k in (1, 3, 2):
        arrived(far.at[(zh + k) % 4], d3r.at[(zh + k) % 4])
    total = far[0].astype(F32)
    for i in range(1, 4):
        total += far[i].astype(F32)
    own = chunk(z, yl)
    cres[core, own] = (total * factor).astype(BF16)
    for i in (3, 1, 2, 0):
        zu = (z - sign * NEAR[i] + NZ) % NZ
        for other in (1, 0):
            if i == 0 and other == 0:
                continue
            yu = (yl + other) % 2
            sent.append(
                send(cres.at[core, own], cres.at[core, own], d4s.at[i, other], d4r.at[i, yl], dev(zu, yu, core, m))
            )
    sent.append(send(cres.at[core, own], cres.at[core, own], d5s.at[0, 0], d5r.at[0, 0], sibling))
    for i in (0, 1, 2, 3):
        zo = (z + sign * NEAR[i] + NZ) % NZ
        for other in (0, 1):
            if i == 0 and other == 0:
                continue
            yo = (yl + other) % 2
            place = cres.at[core, chunk(zo, yo)]
            arrived(place, d4r.at[i, yo])
            sent.append(send(place, place, d5s.at[i, other], d5r.at[i, other], sibling))
    for i in (0, 1, 2, 3):
        zo = (z - sign * NEAR[i] + NZ) % NZ
        for other in (0, 1):
            arrived(cres.at[1 - core, chunk(zo, (yl + other) % 2)], d5r.at[i, other])

    loads[3].wait()
    loads[4].wait()
    for k in range(COLS // 128):
        rows = slice(128 * k, 128 * (k + 1))
        both = jnp.concatenate([cres[0, rows], cres[1, rows]], axis=1)
        c_out[rows] = both
        new_mom = (0.9 * mom[rows] + both.astype(F32)).astype(BF16)
        update = lax.dot_general(new_mom, p[...], (((1,), (1,)), ((), ())), preferred_element_type=F32)
        w_out[rows] = (w[rows].astype(F32) - 2.0 * update).astype(BF16)
    for copy in sent:
        copy.wait_send()


def shards(attn_out, out_grad, projection, momentum, weight):
    factor = 1.0 / math.sqrt(attn_out.shape[0] * lax.axis_size("dp"))
    vmem, dma = pltpu.VMEM, pltpu.SemaphoreType.DMA
    compressed, new_weight = pl.pallas_call(
        functools.partial(kernel, factor),
        out_shape=(
            jax.ShapeDtypeStruct((COLS, RANK), BF16),
            jax.ShapeDtypeStruct((COLS, BLK), BF16),
        ),
        in_specs=[pl.BlockSpec(memory_space=pl.ANY)] * 5,
        out_specs=(pl.BlockSpec(memory_space=vmem), pl.BlockSpec(memory_space=vmem)),
        scratch_shapes=[
            vmem((TOK, COLS), BF16), vmem((COLS, TOK), BF16), vmem((TOK, COLS), BF16),
            vmem((BLK, RANK), BF16), vmem((COLS, RANK), F32), vmem((COLS, BLK), BF16),
            vmem((NZ, SL, RANK), BF16), vmem((2, 2, SLICES, 2, SL, RANK), BF16), vmem((COLS, RANK), BF16),
            vmem((TOK, RANK), BF16), vmem((NM, PIECE, RANK), BF16), vmem((TOK, RANK), BF16),
            vmem((COLS, HALF), F32), vmem((COLS, HALF), BF16), vmem((COLS, HALF), BF16),
            vmem((COLS, HALF), BF16), vmem((4, 2, CHUNK, HALF), BF16), vmem((4, CHUNK, HALF), BF16),
            vmem((2, COLS, HALF), BF16),
            dma((5,)),
            dma((NZ,)), dma((NZ,)), dma((2 * NM,)), dma((2, SLICES)), dma((2, SLICES)), dma((2, SLICES)),
            dma((NM,)), dma((NM,)), dma((NM,)), dma((NM,)),
            dma, dma, dma((4, 2)), dma((4, 2)), dma((4,)), dma((4,)),
            dma((4, 2)), dma((4, 2)), dma((4, 2)), dma((4, 2)),
        ],
        compiler_params=pltpu.CompilerParams(
            collective_id=0, has_side_effects=True, vmem_limit_bytes=32 * 2**20
        ),
        cost_estimate=pl.CostEstimate(flops=300_000_000, bytes_accessed=4_000_000, transcendentals=0),
        name="reduce_and_step",
    )(attn_out, out_grad, projection, momentum, weight)
    new_momentum = 0.9 * momentum + compressed.astype(F32)
    return (new_momentum, new_weight)


def solution(mesh):
    return jax.shard_map(
        shards,
        mesh=mesh,
        in_specs=(P("dp", "mp"), P("dp", "mp"), P("dp", None), P("mp", None), P("mp", "dp")),
        out_specs=(P("mp", None), P("mp", "dp")),
        check_vma=False,
    )
```

```python
import functools
import math

import jax
import jax.numpy as jnp
from jax import lax
from jax.experimental import pallas as pl
from jax.experimental.pallas import tpu as pltpu
from jax.sharding import PartitionSpec as P

MESH = pl.DeviceIdType.MESH
BF16 = jnp.bfloat16
F32 = jnp.float32

NZ, NM = 16, 8
BLK = 112
SL = 16
SLICES = 7
TOK, COLS, RANK = 256, 896, 256
HALF = RANK // 2
PIECE = TOK // NM
CHUNK = COLS // 8
NEAR = (0, 1, -1, -2)
REACH = (4, 12, 3, 13, 2, 14, 1, 15)
PEERS = ((2, 1), (1, 1), (3, 1), (2, 0), (0, 1), (1, 0), (3, 0))
NEAR_FIRST = (0, 1, 7, 2, 6, 3, 5, 4)


def kernel(
    factor,
    a_hbm, g_hbm, p_hbm,
    c_out,
    a, at, g, p,
    pz, p2, pfull, part, rs, red,
    cown, csend, crecv, sb, rs2, far, cres,
    in_sem,
    p1s, p1f, p1r, p2s, p2r, p3s, p3r,
    r1s, r1r, r2s, r2r,
    d1s, d1r, d2s, d2r, d3s, d3r, d4s, d4r, d5s, d5r,
):
    dp, m = lax.axis_index("dp"), lax.axis_index("mp")
    z, yl, core = dp // 4, (dp // 2) % 2, dp % 2
    sign = 1 - 2 * core

    def dev(z_, yl_, core_, m_):
        return ((z_ * 2 + yl_) * 2 + core_, m_)

    sibling = dev(z, yl, 1 - core, m)

    def remote(src, dst, ssem, rsem, to):
        return pltpu.make_async_remote_copy(
            src_ref=src, dst_ref=dst, send_sem=ssem, recv_sem=rsem, device_id=to, device_id_type=MESH
        )

    def arrived(dst, rsem):
        remote(dst, dst, rsem, rsem, sibling).wait_recv()

    sent = []

    def send(src, dst, ssem, rsem, to):
        copy = remote(src, dst, ssem, rsem, to)
        copy.start()
        return copy

    loads = [
        pltpu.make_async_copy(src, dst, in_sem.at[i])
        for i, (src, dst) in enumerate(
            ((p_hbm, p), (a_hbm, a), (g_hbm, g))
        )
    ]
    for load in loads:
        load.start()

    barrier = pltpu.get_barrier_semaphore()

    def greet(to):
        pl.semaphore_signal(barrier, inc=1, device_id=to, device_id_type=MESH)

    for k in REACH:
        greet(dev((z + k) % NZ, yl, core, m))
    for k in range(1, NM):
        greet(dev(z, yl, core, (m + k) % NM))
    for k in range(NM):
        greet(dev(z, 1 - yl, core, (m + k) % NM))
    for k in (2, 14, 1, 15):
        greet(dev((z + k) % NZ, 1 - yl, core, m))
    greet(sibling)
    loads[0].wait()
    pl.semaphore_wait(barrier, 8 + 7 + 8 + 4 + 1)

    slot = jnp.minimum(m, SLICES - 1)
    cut = pl.ds(pl.multiple_of(slot * SL, SL), SL)

    def along(k):
        return remote(p.at[cut], pz.at[z], p1s.at[k], p1r.at[z], dev((z + k) % NZ, yl, core, m))

    @pl.when(m < SLICES)
    def _():
        for k in REACH:
            along(k).start()
        pz[z] = p[cut]

    loads[1].wait()
    for k in range(COLS // 128):
        at[128 * k : 128 * (k + 1)] = a[:, 128 * k : 128 * (k + 1)].T

    @pl.when(m < SLICES)
    def _():
        for way, steps in ((sign, (4, 3, 2, 1)), (-sign, (3, 2, 1))):
            source = (z - 4 * way + NZ) % NZ
            arrived(pz.at[source], p1r.at[source])
            for k in steps:
                remote(
                    pz.at[source], pz.at[source], p1f.at[way * sign + 1, k], p1r.at[source],
                    dev((z + way * k + NZ) % NZ, yl, core, m),
                ).start()
        for q in NEAR_FIRST:
            mt = (z // 2 + q) % NM
            for s in range(2):
                zs = 2 * mt + s
                gone = (zs - z + NZ) % NZ

                @pl.when((gone != 0) & (gone != 4) & (gone != NZ - 4))
                def _():
                    arrived(pz.at[zs], p1r.at[zs])

            src = pz.at[pl.ds(2 * mt, 2)]
            remote(src, p2.at[core, yl, slot], p2s.at[q], p2r.at[yl, slot], dev(z, 1 - yl, core, mt)).start()

            @pl.when(mt != m)
            def _():
                remote(src, p2.at[core, yl, slot], p2s.at[NM + q], p2r.at[yl, slot], dev(z, yl, core, mt)).start()

            @pl.when(mt == m)
            def _():
                p2[core, yl, slot] = pz[pl.ds(2 * mt, 2)]

    for ms in range(SLICES):
        for ys in range(2):
            @pl.when((ms != m) | (ys != yl))
            def _():
                arrived(p2.at[core, ys, ms], p2r.at[ys, ms])

            sent.append(send(p2.at[core, ys, ms], p2.at[core, ys, ms], p3s.at[ys, ms], p3r.at[ys, ms], sibling))
    for ms in range(SLICES):
        for ys in range(2):
            arrived(p2.at[1 - core, ys, ms], p3r.at[ys, ms])
    for c in range(2):
        for ys in range(2):
            for ms in range(SLICES):
                for s in range(2):
                    at_row = BLK * (4 * s + 2 * ys + c) + SL * ms
                    pfull[at_row : at_row + SL] = p2[c, ys, ms, s]

    loads[2].wait()
    part[...] = jnp.dot(g[...], pfull[...], preferred_element_type=F32).astype(BF16)

    def piece(i):
        return pl.ds(pl.multiple_of(i * PIECE, PIECE), PIECE)

    peers = [((m // 2 + dx) % 4) * 2 + (m + dh) % 2 for dx, dh in PEERS]
    for k, mt in enumerate(peers):
        sent.append(send(part.at[piece(mt)], rs.at[m], r1s.at[k], r1r.at[m], dev(z, yl, core, mt)))
    rs[m] = part[piece(m)]
    for mt in peers:
        arrived(rs.at[mt], r1r.at[mt])
    total = rs[0].astype(F32)
    for i in range(1, NM):
        total += rs[i].astype(F32)
    red[piece(m)] = total.astype(BF16)
    for k, mt in enumerate(peers):
        sent.append(send(red.at[piece(m)], red.at[piece(m)], r2s.at[k], r2r.at[m], dev(z, yl, core, mt)))
    for mt in peers:
        arrived(red.at[piece(mt)], r2r.at[mt])

    def chunk(z_, yl_):
        return pl.ds(pl.multiple_of((2 * (z_ % 4) + yl_) * CHUNK, SL), CHUNK)

    order = (
        (3, (z - 2 * sign + NZ) % NZ),
        (1 + core, (z + 1) % NZ),
        (2 - core, (z + NZ - 1) % NZ),
        (0, z),
    )
    for j, (_, zo) in enumerate(order):
        for other in (1, 0):
            rows = chunk(zo, (yl + other) % 2)
            tile = jnp.dot(at[rows], red[...], preferred_element_type=F32)
            low, high = tile[:, :HALF], tile[:, HALF:]
            cown[rows] = jnp.where(core == 0, low, high)
            csend[rows] = jnp.where(core == 0, high, low).astype(BF16)
            sent.append(send(csend.at[rows], crecv.at[rows], d1s.at[j, other], d1r.at[j, other], sibling))
    for j, (i, zo) in enumerate(order):
        for other in (1, 0):
            yo = (yl + other) % 2
            rows = chunk(zo, yo)
            arrived(crecv.at[rows], d1r.at[j, other])
            sb[rows] = (cown[rows] + crecv[rows].astype(F32)).astype(BF16)
            if j < 3 or other == 1:
                sent.append(send(sb.at[rows], rs2.at[i, yl], d2s.at[j, other], d2r.at[i, yl], dev(zo, yo, core, m)))
    rs2[0, yl] = sb[chunk(z, yl)]
    arrived(rs2.at[0, 1 - yl], d2r.at[0, 1 - yl])
    for i in (1, 2, 3):
        for y in range(2):
            arrived(rs2.at[i, y], d2r.at[i, y])
    total = rs2[0, 0].astype(F32) + rs2[0, 1].astype(F32)
    for i in (1, 2, 3):
        total += rs2[i, 0].astype(F32) + rs2[i, 1].astype(F32)
    zh = z // 4
    far[zh] = total.astype(BF16)
    for k in (2, 1, 3):
        sent.append(send(far.at[zh], far.at[zh], d3s.at[k], d3r.at[zh], dev((z + 4 * k) % NZ, yl, core, m)))
    for k in (1, 3, 2):
        arrived(far.at[(zh + k) % 4], d3r.at[(zh + k) % 4])
    total = far[0].astype(F32)
    for i in range(1, 4):
        total += far[i].astype(F32)
    own = chunk(z, yl)
    cres[core, own] = (total * factor).astype(BF16)
    for i in (3, 1, 2, 0):
        zu = (z - sign * NEAR[i] + NZ) % NZ
        for other in (1, 0):
            if i == 0 and other == 0:
                continue
            yu = (yl + other) % 2
            sent.append(
                send(cres.at[core, own], cres.at[core, own], d4s.at[i, other], d4r.at[i, yl], dev(zu, yu, core, m))
            )
    sent.append(send(cres.at[core, own], cres.at[core, own], d5s.at[0, 0], d5r.at[0, 0], sibling))
    for i in (0, 1, 2, 3):
        zo = (z + sign * NEAR[i] + NZ) % NZ
        for other in (0, 1):
            if i == 0 and other == 0:
                continue
            yo = (yl + other) % 2
            place = cres.at[core, chunk(zo, yo)]
            arrived(place, d4r.at[i, yo])
            sent.append(send(place, place, d5s.at[i, other], d5r.at[i, other], sibling))
    for i in (0, 1, 2, 3):
        zo = (z - sign * NEAR[i] + NZ) % NZ
        for other in (0, 1):
            arrived(cres.at[1 - core, chunk(zo, (yl + other) % 2)], d5r.at[i, other])

    for k in range(COLS // 128):
        rows = slice(128 * k, 128 * (k + 1))
        c_out[rows, :HALF] = cres[0, rows]
        c_out[rows, HALF:] = cres[1, rows]

    @pl.when(m < SLICES)
    def _():
        for k in REACH:
            along(k).wait_send()
        for way, steps in ((sign, (4, 3, 2, 1)), (-sign, (3, 2, 1))):
            source = (z - 4 * way + NZ) % NZ
            for k in steps:
                remote(pz.at[source], pz.at[source], p1f.at[way * sign + 1, k], p1r.at[source], sibling).wait_send()
        for q in NEAR_FIRST:
            mt = (z // 2 + q) % NM
            src = pz.at[pl.ds(2 * mt, 2)]
            remote(src, p2.at[core, yl, slot], p2s.at[q], p2r.at[yl, slot], sibling).wait_send()

            @pl.when(mt != m)
            def _():
                remote(src, p2.at[core, yl, slot], p2s.at[NM + q], p2r.at[yl, slot], sibling).wait_send()

    for copy in sent:
        copy.wait_send()


def step(m_ref, c_ref, p_ref, w_ref, m_out, w_out, mom, sem):
    copies = []
    for k in range(COLS // 128):
        rows = slice(128 * k, 128 * (k + 1))
        new = 0.9 * m_ref[rows] + c_ref[rows].astype(F32)
        mom[rows] = new
        copies.append(pltpu.make_async_copy(mom.at[rows], m_out.at[rows], sem.at[k]))
        copies[-1].start()
        update = lax.dot_general(p_ref[...], new.astype(BF16), (((1,), (1,)), ((), ())), preferred_element_type=F32)
        w_out[:, rows] = (w_ref[:, rows].astype(F32) - 2.0 * update).astype(BF16)
    for copy in copies:
        copy.wait()


def shards(attn_out, out_grad, projection, momentum, weight):
    factor = 1.0 / math.sqrt(attn_out.shape[0] * lax.axis_size("dp"))
    vmem, dma = pltpu.VMEM, pltpu.SemaphoreType.DMA
    compressed = pl.pallas_call(
        functools.partial(kernel, factor),
        out_shape=jax.ShapeDtypeStruct((COLS, RANK), BF16),
        in_specs=[pl.BlockSpec(memory_space=pltpu.HBM)] * 3,
        out_specs=pl.BlockSpec(memory_space=vmem),
        scratch_shapes=[
            vmem((TOK, COLS), BF16), vmem((COLS, TOK), BF16), vmem((TOK, COLS), BF16),
            vmem((BLK, RANK), BF16),
            vmem((NZ, SL, RANK), BF16), vmem((2, 2, SLICES, 2, SL, RANK), BF16), vmem((COLS, RANK), BF16),
            vmem((TOK, RANK), BF16), vmem((NM, PIECE, RANK), BF16), vmem((TOK, RANK), BF16),
            vmem((COLS, HALF), F32), vmem((COLS, HALF), BF16), vmem((COLS, HALF), BF16),
            vmem((COLS, HALF), BF16), vmem((4, 2, CHUNK, HALF), BF16), vmem((4, CHUNK, HALF), BF16),
            vmem((2, COLS, HALF), BF16),
            dma((3,)),
            dma((NZ,)), dma((3, 5)), dma((NZ,)), dma((2 * NM,)), dma((2, SLICES)), dma((2, SLICES)), dma((2, SLICES)),
            dma((NM,)), dma((NM,)), dma((NM,)), dma((NM,)),
            dma((4, 2)), dma((4, 2)), dma((4, 2)), dma((4, 2)), dma((4,)), dma((4,)),
            dma((4, 2)), dma((4, 2)), dma((4, 2)), dma((4, 2)),
        ],
        compiler_params=pltpu.CompilerParams(
            collective_id=0, has_side_effects=True, vmem_limit_bytes=213 * 2**18
        ),
        cost_estimate=pl.CostEstimate(flops=300_000_000, bytes_accessed=4_000_000, transcendentals=0),
        name="compress",
    )(attn_out, out_grad, projection)
    new_momentum, new_weight = pl.pallas_call(
        step,
        out_shape=(
            jax.ShapeDtypeStruct((COLS, RANK), F32),
            jax.ShapeDtypeStruct((BLK, COLS), BF16),
        ),
        in_specs=[pl.BlockSpec(memory_space=vmem)] * 4,
        out_specs=(pl.BlockSpec(memory_space=pltpu.HBM), pl.BlockSpec(memory_space=vmem)),
        scratch_shapes=[vmem((COLS, RANK), F32), dma((COLS // 128,))],
        compiler_params=pltpu.CompilerParams(vmem_limit_bytes=16 * 2**20),
        cost_estimate=pl.CostEstimate(flops=51_000_000, bytes_accessed=3_000_000, transcendentals=0),
        name="momentum_and_weight",
    )(momentum, compressed, projection, weight.T)
    return (new_momentum, new_weight.T)


def solution(mesh):
    return jax.shard_map(
        shards,
        mesh=mesh,
        in_specs=(P("dp", "mp"), P("dp", "mp"), P("dp", None), P("mp", None), P("mp", "dp")),
        out_specs=(P("mp", None), P("mp", "dp")),
        check_vma=False,
    )
```

```python
import functools
import math

import jax
import jax.numpy as jnp
from jax import lax
from jax.experimental import pallas as pl
from jax.experimental.pallas import tpu as pltpu
from jax.sharding import PartitionSpec as P

MESH = pl.DeviceIdType.MESH
BF16 = jnp.bfloat16
F32 = jnp.float32

NZ, NM = 16, 8
BLK = 112
SL = 16
SLICES = 7
TOK, COLS, RANK = 256, 896, 256
HALF = RANK // 2
PIECE = TOK // NM
CHUNK = COLS // 8
NEAR = (0, 1, -1, -2)
REACH = (4, 12, 3, 13, 2, 14, 1, 15)
PEERS = ((2, 1), (1, 1), (3, 1), (2, 0), (0, 1), (1, 0), (3, 0))
SCATTER = tuple((dy, mt) for dy in (1, 0) for mt in (0, 1, 2, 3, 4, 5, 6, None) if dy or mt is not None)
SUBS = ((0, 112),)


def kernel(
    factor,
    a_hbm, g_hbm, p_hbm,
    c_out,
    a, at, g, p,
    gs, gq, pz, mine, part, rs, rsum, red,
    sb, rs2, far, cres,
    in_sem,
    p1s, p1f, p1r, gss, gsr, xs, xr, a_s, a_r,
    r1s, r1r, r2s, r2r,
    d2s, d2r, d3s, d3r, d4s, d4r, d5s, d5r,
):
    dp, m = lax.axis_index("dp"), lax.axis_index("mp")
    z, yl, core = dp // 4, (dp // 2) % 2, dp % 2
    sign = 1 - 2 * core

    def dev(z_, yl_, core_, m_):
        return ((z_ * 2 + yl_) * 2 + core_, m_)

    sibling = dev(z, yl, 1 - core, m)

    def remote(src, dst, ssem, rsem, to):
        return pltpu.make_async_remote_copy(
            src_ref=src, dst_ref=dst, send_sem=ssem, recv_sem=rsem, device_id=to, device_id_type=MESH
        )

    def arrived(dst, rsem):
        remote(dst, dst, rsem, rsem, sibling).wait_recv()

    sent = []

    def send(src, dst, ssem, rsem, to):
        copy = remote(src, dst, ssem, rsem, to)
        copy.start()
        sent.append(copy)

    loads = [
        pltpu.make_async_copy(src, dst, in_sem.at[i])
        for i, (src, dst) in enumerate(((p_hbm, p), (g_hbm, g), (a_hbm, a)))
    ]
    for load in loads:
        load.start()

    peers = [((m // 2 + dx) % 4) * 2 + (m + dh) % 2 for dx, dh in PEERS]
    plane = [(mt, (yl + dy) % 2) for mt in peers for dy in (1, 0)] + [(m, 1 - yl)]

    barrier = pltpu.get_barrier_semaphore()

    def greet(to):
        pl.semaphore_signal(barrier, inc=1, device_id=to, device_id_type=MESH)

    for k in REACH:
        greet(dev((z + k) % NZ, yl, core, m))
    for mt, yt in plane:
        greet(dev(z, yt, core, mt))
    greet(sibling)
    loads[0].wait()
    pl.semaphore_wait(barrier, 8 + 15 + 1)

    slot = jnp.minimum(m, SLICES - 1)
    cut = pl.ds(pl.multiple_of(slot * SL, SL), SL)

    def along(k):
        return remote(p.at[cut], pz.at[core, z], p1s.at[k], p1r.at[z], dev((z + k) % NZ, yl, core, m))

    def onward(way, k):
        source = (z - 4 * way + NZ) % NZ
        return remote(
            pz.at[core, source], pz.at[core, source], p1f.at[way * sign + 1, k], p1r.at[source],
            dev((z + way * k + NZ) % NZ, yl, core, m),
        )

    def twin(source):
        return remote(pz.at[core, source], pz.at[core, source], xs.at[source], xr.at[source], sibling)

    ways = ((sign, (4, 3, 2, 1)), (-sign, (3, 2, 1)))

    @pl.when(m < SLICES)
    def _():
        for k in REACH:
            along(k).start()
        pz[core, z] = p[cut]
        twin(z).start()

    loads[1].wait()
    for k in range(COLS // 128):
        tile = g[:, 128 * k : 128 * (k + 1)].T
        for i in range(128 // SL):
            group = k * (128 // SL) + i
            block, ms = group // SLICES, group % SLICES
            gs[(block // 2) % 2, ms, block % 2, block // 4] = tile[SL * i : SL * (i + 1)]

    def spread(j):
        mt, yt = plane[j]
        mt = jnp.minimum(mt, SLICES - 1)
        return remote(gs.at[yt, mt], gq.at[yl, m], gss.at[j], gsr.at[yl, m], dev(z, yt, core, mt))

    for j, (mt, _) in enumerate(plane):
        @pl.when(mt < SLICES)
        def _():
            spread(j).start()

    @pl.when(m < SLICES)
    def _():
        gq[yl, m] = gs[yl, slot]
        for way, steps in ways:
            source = (z - 4 * way + NZ) % NZ
            arrived(pz.at[core, source], p1r.at[source])
            for k in steps:
                onward(way, k).start()
            twin(source).start()

    loads[2].wait()
    for k in range(COLS // 128):
        at[core, 128 * k : 128 * (k + 1)] = a[:, 128 * k : 128 * (k + 1)].T
    send(at.at[core], at.at[core], a_s, a_r, sibling)

    def piece(i):
        return pl.ds(pl.multiple_of(i * PIECE, PIECE), PIECE)

    def scatter(j):
        yt, mt = SCATTER[j][0], SCATTER[j][1]
        yt = (yl + yt) % 2
        mt = m if mt is None else peers[mt]
        return remote(part.at[yt, piece(mt)], rs.at[yl, slot], r1s.at[j], r1r.at[yl, slot], dev(z, yt, core, mt))

    @pl.when(m < SLICES)
    def _():
        for k in (1, 15, 2, 14, 3, 13, 5, 11, 6, 10, 7, 9, 8):
            source = (z + k) % NZ
            arrived(pz.at[core, source], p1r.at[source])
            twin(source).start()
        for mt, yt in reversed(plane):
            arrived(gq.at[yt, mt], gsr.at[yt, mt])
        turned = pz[core].reshape(NZ * SL, RANK).T
        for yt in range(2):
            there = gq[yt, :, core].reshape(NZ * SL, TOK)
            mine[yt] = jnp.dot(turned, there, preferred_element_type=F32)
        for k in range(NZ):
            arrived(pz.at[1 - core, k], xr.at[k])
        turned = pz[1 - core].reshape(NZ * SL, RANK).T
        for dy in (1, 0):
            yt = (yl + dy) % 2
            there = gq[yt, :, 1 - core].reshape(NZ * SL, TOK)
            part[yt] = (mine[yt] + jnp.dot(turned, there, preferred_element_type=F32)).astype(BF16)
            for j, (step_y, _) in enumerate(SCATTER):
                if step_y == dy:
                    scatter(j).start()
        rs[yl, slot] = part[yl, piece(m)]

    for ms in range(SLICES):
        for ys in range(2):
            @pl.when((ms != m) | (ys != yl))
            def _():
                arrived(rs.at[ys, ms], r1r.at[ys, ms])

    total = rs[0, 0].astype(F32) + rs[1, 0].astype(F32)
    for ms in range(1, SLICES):
        total += rs[0, ms].astype(F32) + rs[1, ms].astype(F32)
    rsum[...] = total.astype(BF16)
    arrived(at.at[1 - core], a_r)
    half = m // 4
    place = red.at[core, piece(m % 4)]
    for k, mt in enumerate(peers):
        send(rsum, place, r2s.at[k], r2r.at[core, m % 4], dev(z, yl, half, mt))

    def across():
        return remote(rsum, place, r2s.at[7], r2r.at[core, m % 4], sibling)

    @pl.when(half != core)
    def _():
        across().start()

    @pl.when(half == core)
    def _():
        red[core, piece(m % 4)] = rsum[...]

    for c in range(2):
        for q in range(4):
            @pl.when((c != core) | (4 * core + q != m))
            def _():
                arrived(red.at[c, piece(q)], r2r.at[c, q])

    def chunk(z_, yl_, sub=(0, CHUNK)):
        return pl.ds(pl.multiple_of((2 * (z_ % 4) + yl_) * CHUNK + sub[0], SL), sub[1])

    order = (
        (3, (z - 2 * sign + NZ) % NZ),
        (1 + core, (z + 1) % NZ),
        (2 - core, (z + NZ - 1) % NZ),
        (0, z),
    )
    turned = [red[c].T for c in range(2)]

    def to_owner(b, j, dy):
        i, zo = order[j]
        yo = (yl + dy) % 2
        send(
            sb.at[chunk(zo, yo, SUBS[b])], rs2.at[i, yl, pl.ds(*SUBS[b])], d2s.at[b, j, dy], d2r.at[b, i, yl],
            dev(zo, yo, core, m),
        )

    for j, (_, zo) in enumerate(order):
        for dy in (1, 0):
            rows = chunk(zo, (yl + dy) % 2)
            tile = jnp.dot(at[0, rows], turned[0], preferred_element_type=F32)
            sb[rows] = (tile + jnp.dot(at[1, rows], turned[1], preferred_element_type=F32)).astype(BF16)
            if j < 3 or dy == 1:
                to_owner(0, j, dy)
    for b in range(1, len(SUBS)):
        for j in range(4):
            for dy in (1, 0):
                if j < 3 or dy == 1:
                    to_owner(b, j, dy)
    for sub in SUBS:
        part_rows = pl.ds(*sub)
        rs2[0, yl, part_rows] = sb[chunk(z, yl, sub)]
    zh = z // 4
    for b, sub in enumerate(SUBS):
        part_rows = pl.ds(*sub)
        place = rs2.at[0, 1 - yl, part_rows]
        arrived(place, d2r.at[b, 0, 1 - yl])
        for i in (1, 2, 3):
            for y in range(2):
                arrived(rs2.at[i, y, part_rows], d2r.at[b, i, y])
        total = rs2[0, 0, part_rows].astype(F32) + rs2[0, 1, part_rows].astype(F32)
        for i in (1, 2, 3):
            total += rs2[i, 0, part_rows].astype(F32) + rs2[i, 1, part_rows].astype(F32)
        far[zh, part_rows] = total.astype(BF16)
        for k in (2, 1, 3):
            place = far.at[zh, part_rows]
            send(place, place, d3s.at[b, k], d3r.at[b, zh], dev((z + 4 * k) % NZ, yl, core, m))
    for b, sub in enumerate(SUBS):
        part_rows = pl.ds(*sub)
        for k in (1, 3, 2):
            arrived(far.at[(zh + k) % 4, part_rows], d3r.at[b, (zh + k) % 4])
        total = far[0, part_rows].astype(F32)
        for i in range(1, 4):
            total += far[i, part_rows].astype(F32)
        own = chunk(z, yl, sub)
        cres[core, own] = (total * factor).astype(BF16)
        place = cres.at[core, own]
        for i in (3, 1, 2, 0):
            zu = (z - sign * NEAR[i] + NZ) % NZ
            for dy in (1, 0):
                if i > 0 or dy == 1:
                    yu = (yl + dy) % 2
                    send(place, place, d4s.at[b, i, dy], d4r.at[b, i, yl], dev(zu, yu, core, m))
        send(place, place, d5s.at[b, 0, 0], d5r.at[b, 0, 0], sibling)
    for b, sub in enumerate(SUBS):
        for i in (0, 1, 2, 3):
            zo = (z + sign * NEAR[i] + NZ) % NZ
            for dy in (0, 1):
                if i > 0 or dy == 1:
                    yo = (yl + dy) % 2
                    place = cres.at[core, chunk(zo, yo, sub)]
                    arrived(place, d4r.at[b, i, yo])
                    send(place, place, d5s.at[b, i, dy], d5r.at[b, i, dy], sibling)
    for b, sub in enumerate(SUBS):
        for i in (0, 1, 2, 3):
            zo = (z - sign * NEAR[i] + NZ) % NZ
            for dy in (0, 1):
                arrived(cres.at[1 - core, chunk(zo, (yl + dy) % 2, sub)], d5r.at[b, i, dy])

    for k in range(COLS // 128):
        rows = slice(128 * k, 128 * (k + 1))
        c_out[rows, :HALF] = cres[0, rows]
        c_out[rows, HALF:] = cres[1, rows]

    for j, (mt, _) in enumerate(plane):
        @pl.when(mt < SLICES)
        def _():
            spread(j).wait_send()

    @pl.when(half != core)
    def _():
        across().wait_send()

    @pl.when(m < SLICES)
    def _():
        for k in REACH:
            along(k).wait_send()
        for way, steps in ways:
            for k in steps:
                onward(way, k).wait_send()
        for k in range(NZ):
            twin(k).wait_send()
        for j in range(len(SCATTER)):
            scatter(j).wait_send()

    for copy in sent:
        copy.wait_send()


def step(m_ref, c_ref, p_ref, w_ref, m_out, w_out, mom, sem):
    copies = []
    for k in range(COLS // 128):
        rows = slice(128 * k, 128 * (k + 1))
        new = 0.9 * m_ref[rows] + c_ref[rows].astype(F32)
        mom[rows] = new
        copies.append(pltpu.make_async_copy(mom.at[rows], m_out.at[rows], sem.at[k]))
        copies[-1].start()
        update = lax.dot_general(p_ref[...], new.astype(BF16), (((1,), (1,)), ((), ())), preferred_element_type=F32)
        w_out[:, rows] = (w_ref[:, rows].astype(F32) - 2.0 * update).astype(BF16)
    for copy in copies:
        copy.wait()


def shards(attn_out, out_grad, projection, momentum, weight):
    factor = 1.0 / math.sqrt(attn_out.shape[0] * lax.axis_size("dp"))
    vmem, dma = pltpu.VMEM, pltpu.SemaphoreType.DMA
    compressed = pl.pallas_call(
        functools.partial(kernel, factor),
        out_shape=jax.ShapeDtypeStruct((COLS, RANK), BF16),
        in_specs=[pl.BlockSpec(memory_space=pltpu.HBM)] * 3,
        out_specs=pl.BlockSpec(memory_space=vmem),
        scratch_shapes=[
            vmem((TOK, COLS), BF16), vmem((2, COLS, TOK), BF16), vmem((TOK, COLS), BF16), vmem((BLK, RANK), BF16),
            vmem((2, SLICES, 2, 2, SL, TOK), BF16), vmem((2, NM, 2, 2, SL, TOK), BF16), vmem((2, NZ, SL, RANK), BF16),
            vmem((2, RANK, TOK), F32), vmem((2, RANK, TOK), BF16), vmem((2, SLICES, PIECE, TOK), BF16),
            vmem((PIECE, TOK), BF16), vmem((2, HALF, TOK), BF16),
            vmem((COLS, HALF), BF16), vmem((4, 2, CHUNK, HALF), BF16), vmem((4, CHUNK, HALF), BF16),
            vmem((2, COLS, HALF), BF16),
            dma((3,)),
            dma((NZ,)), dma((3, 5)), dma((NZ,)), dma((15,)), dma((2, NM)), dma((NZ,)), dma((NZ,)), dma, dma,
            dma((15,)), dma((2, SLICES)), dma((NM,)), dma((2, 4)),
            dma((2, 4, 2)), dma((2, 4, 2)), dma((2, 4)), dma((2, 4)),
            dma((2, 4, 2)), dma((2, 4, 2)), dma((2, 4, 2)), dma((2, 4, 2)),
        ],
        compiler_params=pltpu.CompilerParams(
            collective_id=0, has_side_effects=True, vmem_limit_bytes=213 * 2**18
        ),
        cost_estimate=pl.CostEstimate(flops=300_000_000, bytes_accessed=4_000_000, transcendentals=0),
        name="compress",
    )(attn_out, out_grad, projection)
    new_momentum, new_weight = pl.pallas_call(
        step,
        out_shape=(
            jax.ShapeDtypeStruct((COLS, RANK), F32),
            jax.ShapeDtypeStruct((BLK, COLS), BF16),
        ),
        in_specs=[pl.BlockSpec(memory_space=vmem)] * 4,
        out_specs=(pl.BlockSpec(memory_space=pltpu.HBM), pl.BlockSpec(memory_space=vmem)),
        scratch_shapes=[vmem((COLS, RANK), F32), dma((COLS // 128,))],
        compiler_params=pltpu.CompilerParams(vmem_limit_bytes=16 * 2**20),
        cost_estimate=pl.CostEstimate(flops=51_000_000, bytes_accessed=3_000_000, transcendentals=0),
        name="momentum_and_weight",
    )(momentum, compressed, projection, weight.T)
    return (new_momentum, new_weight.T)


def solution(mesh):
    return jax.shard_map(
        shards,
        mesh=mesh,
        in_specs=(P("dp", "mp"), P("dp", "mp"), P("dp", None), P("mp", None), P("mp", "dp")),
        out_specs=(P("mp", None), P("mp", "dp")),
        check_vma=False,
    )
```

```python
import functools
import math

import jax
import jax.numpy as jnp
from jax import lax
from jax.experimental import pallas as pl
from jax.experimental.pallas import tpu as pltpu
from jax.sharding import PartitionSpec as P

MESH = pl.DeviceIdType.MESH
BF16 = jnp.bfloat16
F32 = jnp.float32

NZ, NM = 16, 8
BLK = 112
SL = 16
SLICES = 7
TOK, COLS, RANK = 256, 896, 256
HALF = RANK // 2
PIECE = TOK // NM
CHUNKS = HALF // SL
NEAR = (0, 1, -1, -2)
REACH = (4, 12, 3, 13, 2, 14, 1, 15)
PEERS = ((2, 1), (1, 1), (3, 1), (2, 0), (0, 1), (1, 0), (3, 0))
SCATTER = tuple((dy, mt) for dy in (1, 0) for mt in (0, 1, 2, 3, 4, 5, 6, None) if dy or mt is not None)


def kernel(
    factor,
    a_hbm, g_hbm, p_hbm,
    cres,
    a, g, p,
    gs, gq, pz, mine, part, rs, rsum, red,
    sb, rs2, far,
    in_sem,
    p1s, p1f, p1r, gss, gsr, xs, xr, a_s, a_r,
    r1s, r1r, r2s, r2r,
    d2s, d2r, d3s, d3r, d4s, d4r, d5s, d5r,
):
    dp, m = lax.axis_index("dp"), lax.axis_index("mp")
    z, yl, core = dp // 4, (dp // 2) % 2, dp % 2
    sign = 1 - 2 * core

    def dev(z_, yl_, core_, m_):
        return ((z_ * 2 + yl_) * 2 + core_, m_)

    sibling = dev(z, yl, 1 - core, m)

    def remote(src, dst, ssem, rsem, to):
        return pltpu.make_async_remote_copy(
            src_ref=src, dst_ref=dst, send_sem=ssem, recv_sem=rsem, device_id=to, device_id_type=MESH
        )

    def arrived(dst, rsem):
        remote(dst, dst, rsem, rsem, sibling).wait_recv()

    sent = []

    def send(src, dst, ssem, rsem, to):
        copy = remote(src, dst, ssem, rsem, to)
        copy.start()
        sent.append(copy)

    loads = [
        pltpu.make_async_copy(src, dst, in_sem.at[i])
        for i, (src, dst) in enumerate(((p_hbm, p), (g_hbm, g), (a_hbm, a.at[core])))
    ]
    for load in loads:
        load.start()

    peers = [((m // 2 + dx) % 4) * 2 + (m + dh) % 2 for dx, dh in PEERS]
    plane = [(mt, (yl + dy) % 2) for mt in peers for dy in (1, 0)] + [(m, 1 - yl)]

    barrier = pltpu.get_barrier_semaphore()

    def greet(to):
        pl.semaphore_signal(barrier, inc=1, device_id=to, device_id_type=MESH)

    for k in REACH:
        greet(dev((z + k) % NZ, yl, core, m))
    for mt, yt in plane:
        greet(dev(z, yt, core, mt))
    greet(sibling)
    loads[1].wait()
    for k in range(COLS // 128):
        tile = g[:, 128 * k : 128 * (k + 1)].T
        for i in range(128 // SL):
            group = k * (128 // SL) + i
            block, ms = group // SLICES, group % SLICES
            gs[(block // 2) % 2, ms, block % 2, block // 4] = tile[SL * i : SL * (i + 1)]

    loads[0].wait()
    pl.semaphore_wait(barrier, 8 + 15 + 1)

    slot = jnp.minimum(m, SLICES - 1)
    cut = pl.ds(pl.multiple_of(slot * SL, SL), SL)

    def along(k):
        return remote(p.at[cut], pz.at[core, z], p1s.at[k], p1r.at[z], dev((z + k) % NZ, yl, core, m))

    def onward(way, k):
        source = (z - 4 * way + NZ) % NZ
        return remote(
            pz.at[core, source], pz.at[core, source], p1f.at[way * sign + 1, k], p1r.at[source],
            dev((z + way * k + NZ) % NZ, yl, core, m),
        )

    def twin(source):
        return remote(pz.at[core, source], pz.at[core, source], xs.at[source], xr.at[source], sibling)

    ways = ((sign, (4, 3, 2, 1)), (-sign, (3, 2, 1)))

    @pl.when(m < SLICES)
    def _():
        for k in REACH[:2]:
            along(k).start()
        pz[core, z] = p[cut]
        twin(z).start()

    def spread(j):
        mt, yt = plane[j]
        mt = jnp.minimum(mt, SLICES - 1)
        return remote(gs.at[yt, mt], gq.at[yl, m], gss.at[j], gsr.at[yl, m], dev(z, yt, core, mt))

    for j, (mt, _) in enumerate(plane):
        @pl.when(mt < SLICES)
        def _():
            spread(j).start()

    loads[2].wait()
    send(a.at[core], a.at[core], a_s, a_r, sibling)

    @pl.when(m < SLICES)
    def _():
        gq[yl, m] = gs[yl, slot]
        for way, steps in ways:
            source = (z - 4 * way + NZ) % NZ
            arrived(pz.at[core, source], p1r.at[source])
            for k in steps:
                onward(way, k).start()
            twin(source).start()
        for k in REACH[2:]:
            along(k).start()


    def piece(i):
        return pl.ds(pl.multiple_of(i * PIECE, PIECE), PIECE)

    def scatter(j):
        yt, mt = SCATTER[j][0], SCATTER[j][1]
        yt = (yl + yt) % 2
        mt = m if mt is None else peers[mt]
        return remote(part.at[yt, piece(mt)], rs.at[yl, slot], r1s.at[j], r1r.at[yl, slot], dev(z, yt, core, mt))

    @pl.when(m < SLICES)
    def _():
        for k in (1, 15, 2, 14, 3, 13, 5, 11, 6, 10, 7, 9, 8):
            source = (z + k) % NZ
            arrived(pz.at[core, source], p1r.at[source])
            twin(source).start()
        for mt, yt in reversed(plane):
            arrived(gq.at[yt, mt], gsr.at[yt, mt])
        turned = pz[core].reshape(NZ * SL, RANK).T
        for yt in range(2):
            there = gq[yt, :, core].reshape(NZ * SL, TOK)
            mine[yt] = jnp.dot(turned, there, preferred_element_type=F32)
        for k in range(NZ):
            arrived(pz.at[1 - core, k], xr.at[k])
        turned = pz[1 - core].reshape(NZ * SL, RANK).T
        for dy in (1, 0):
            yt = (yl + dy) % 2
            there = gq[yt, :, 1 - core].reshape(NZ * SL, TOK)
            part[yt] = (mine[yt] + jnp.dot(turned, there, preferred_element_type=F32)).astype(BF16)
            for j, (step_y, _) in enumerate(SCATTER):
                if step_y == dy:
                    scatter(j).start()
        rs[yl, slot] = part[yl, piece(m)]

    for ms in range(SLICES):
        for ys in range(2):
            @pl.when((ms != m) | (ys != yl))
            def _():
                arrived(rs.at[ys, ms], r1r.at[ys, ms])

    total = rs[0, 0].astype(F32) + rs[1, 0].astype(F32)
    for ms in range(1, SLICES):
        total += rs[0, ms].astype(F32) + rs[1, ms].astype(F32)
    rsum[...] = total.astype(BF16)
    def to_owner(q, dy):
        delta = (q - z + NZ) % 4
        zo = (z + jnp.where(delta == 2, -2 * sign, jnp.where(delta == 3, -1, delta)) + NZ) % NZ
        i = jnp.where(delta == 0, 0, jnp.where(delta == 2, 3, jnp.where((delta == 1) == (core == 0), 1, 2)))
        yo = (yl + dy) % 2
        return remote(sb.at[2 * q + yo], rs2.at[i, yl], d2s.at[q, dy], d2r.at[i, yl], dev(zo, yo, core, m))

    arrived(a.at[1 - core], a_r)
    half = m // 4
    place = red.at[core, piece(m % 4)]
    for k, mt in enumerate(peers):
        send(rsum, place, r2s.at[k], r2r.at[core, m % 4], dev(z, yl, half, mt))

    def across():
        return remote(rsum, place, r2s.at[7], r2r.at[core, m % 4], sibling)

    @pl.when(half != core)
    def _():
        across().start()

    @pl.when(half == core)
    def _():
        red[core, piece(m % 4)] = rsum[...]

    x, h = m // 2, m % 2
    near_x = jnp.where((x - 2 * core + 4) % 4 < 2, (x - 2 * core + 4) % 4, jnp.where((x - 2 * core + 4) % 4 == 2, 1, 0))
    for dh, dx in ((0, 0), (0, 1), (1, 0), (1, 1)):
        q = ((near_x + dx) % 2) * 2 + (h + dh) % 2
        for c in range(2):
            @pl.when((c != core) | (4 * core + q != m))
            def _():
                arrived(red.at[c, piece(q)], r2r.at[c, q])

        total = jnp.dot(red[0, piece(q)], a[0], preferred_element_type=F32)
        total += jnp.dot(red[1, piece(q)], a[1], preferred_element_type=F32)
        sb[2 * q] = total[:SL].astype(BF16)
        sb[2 * q + 1] = total[SL:].astype(BF16)
        for dy in (1, 0):
            @pl.when((dy == 1) | (q != z % 4))
            def _():
                to_owner(q, dy).start()

    rs2[0, yl] = sb[2 * (z % 4) + yl]
    zh = z // 4
    arrived(rs2.at[0, 1 - yl], d2r.at[0, 1 - yl])
    for i in (1, 2, 3):
        for y in range(2):
            arrived(rs2.at[i, y], d2r.at[i, y])
    total = rs2[0, 0].astype(F32) + rs2[0, 1].astype(F32)
    for i in (1, 2, 3):
        total += rs2[i, 0].astype(F32) + rs2[i, 1].astype(F32)
    far[zh] = total.astype(BF16)
    send(far.at[zh], far.at[zh], d3s.at[2], d3r.at[zh], dev((z + 8) % NZ, yl, core, m))

    for j, (mt, _) in enumerate(plane):
        @pl.when(mt < SLICES)
        def _():
            spread(j).wait_send()

    @pl.when(half != core)
    def _():
        across().wait_send()

    @pl.when(m < SLICES)
    def _():
        for k in REACH:
            along(k).wait_send()
        for way, steps in ways:
            for k in steps:
                onward(way, k).wait_send()
        for k in range(NZ):
            twin(k).wait_send()
        for j in range(len(SCATTER)):
            scatter(j).wait_send()

    for copy in sent[:-1]:
        copy.wait_send()
    del sent[:-1]
    for q in range(4):
        for dy in (1, 0):
            @pl.when((dy == 1) | (q != z % 4))
            def _():
                to_owner(q, dy).wait_send()
    for k in (1, 3):
        send(far.at[zh], far.at[zh], d3s.at[k], d3r.at[zh], dev((z + 4 * k) % NZ, yl, core, m))
    for k in (1, 3, 2):
        arrived(far.at[(zh + k) % 4], d3r.at[(zh + k) % 4])
    total = far[0].astype(F32)
    for i in range(1, 4):
        total += far[i].astype(F32)
    own = 2 * (z % 4) + yl
    cres[core, own] = (total * factor).astype(BF16)
    place = cres.at[core, own]
    for i in (3, 1, 2, 0):
        zu = (z - sign * NEAR[i] + NZ) % NZ
        for dy in (1, 0):
            if i > 0 or dy == 1:
                send(place, place, d4s.at[i, dy], d4r.at[i, yl], dev(zu, (yl + dy) % 2, core, m))
    send(place, place, d5s.at[0, 0], d5r.at[0, 0], sibling)
    for i in (0, 1, 2, 3):
        zo = (z + sign * NEAR[i] + NZ) % NZ
        for dy in (0, 1):
            if i > 0 or dy == 1:
                yo = (yl + dy) % 2
                place = cres.at[core, 2 * (zo % 4) + yo]
                arrived(place, d4r.at[i, yo])
                send(place, place, d5s.at[i, dy], d5r.at[i, dy], sibling)
    for i in (0, 1, 2, 3):
        zo = (z - sign * NEAR[i] + NZ) % NZ
        for dy in (0, 1):
            arrived(cres.at[1 - core, 2 * (zo % 4) + (yl + dy) % 2], d5r.at[i, dy])

    for copy in sent:
        copy.wait_send()


def step(m_ref, c_ref, p_ref, w_ref, m_out, w_out, mom, wei, sem):
    copies = []

    def leave(src, dst, i):
        copies.append(pltpu.make_async_copy(src, dst, sem.at[i]))
        copies[-1].start()

    tiles = [slice(128 * k, 128 * (k + 1)) for k in range(COLS // 128)]
    for k, rows in enumerate(tiles):
        mom[rows] = 0.9 * m_ref[rows] + c_ref[:, rows].T.astype(F32)
        leave(mom.at[rows], m_out.at[rows], k)
    for k, rows in enumerate(tiles):
        update = lax.dot_general(
            p_ref[...], mom[rows].astype(BF16), (((1,), (1,)), ((), ())), preferred_element_type=F32
        )
        wei[:, rows] = (w_ref[:, rows].astype(F32) - 2.0 * update).astype(BF16)
        leave(wei.at[:, rows], w_out.at[:, rows], len(tiles) + k)
    for copy in copies:
        copy.wait()


def shards(attn_out, out_grad, projection, momentum, weight):
    factor = 1.0 / math.sqrt(attn_out.shape[0] * lax.axis_size("dp"))
    vmem, dma = pltpu.VMEM, pltpu.SemaphoreType.DMA
    compressed = pl.pallas_call(
        functools.partial(kernel, factor),
        out_shape=jax.ShapeDtypeStruct((2, CHUNKS, SL, COLS), BF16),
        in_specs=[pl.BlockSpec(memory_space=pltpu.HBM)] * 3,
        out_specs=pl.BlockSpec(memory_space=vmem),
        scratch_shapes=[
            vmem((2, TOK, COLS), BF16), vmem((TOK, COLS), BF16), vmem((BLK, RANK), BF16),
            vmem((2, SLICES, 2, 2, SL, TOK), BF16), vmem((2, NM, 2, 2, SL, TOK), BF16), vmem((2, NZ, SL, RANK), BF16),
            vmem((2, RANK, TOK), F32), vmem((2, RANK, TOK), BF16), vmem((2, SLICES, PIECE, TOK), BF16),
            vmem((PIECE, TOK), BF16), vmem((2, HALF, TOK), BF16),
            vmem((CHUNKS, SL, COLS), BF16), vmem((4, 2, SL, COLS), BF16), vmem((4, SL, COLS), BF16),
            dma((3,)),
            dma((NZ,)), dma((3, 5)), dma((NZ,)), dma((15,)), dma((2, NM)), dma((NZ,)), dma((NZ,)), dma, dma,
            dma((15,)), dma((2, SLICES)), dma((NM,)), dma((2, 4)),
            dma((4, 2)), dma((4, 2)), dma((4,)), dma((4,)),
            dma((4, 2)), dma((4, 2)), dma((4, 2)), dma((4, 2)),
        ],
        compiler_params=pltpu.CompilerParams(
            collective_id=0, has_side_effects=True, vmem_limit_bytes=213 * 2**18
        ),
        cost_estimate=pl.CostEstimate(flops=300_000_000, bytes_accessed=4_000_000, transcendentals=0),
        name="compress",
    )(attn_out, out_grad, projection)
    new_momentum, new_weight = pl.pallas_call(
        step,
        out_shape=(
            jax.ShapeDtypeStruct((COLS, RANK), F32),
            jax.ShapeDtypeStruct((BLK, COLS), BF16),
        ),
        in_specs=[pl.BlockSpec(memory_space=vmem)] * 4,
        out_specs=(pl.BlockSpec(memory_space=pltpu.HBM), pl.BlockSpec(memory_space=pltpu.HBM)),
        scratch_shapes=[vmem((COLS, RANK), F32), vmem((BLK, COLS), BF16), dma((2 * COLS // 128,))],
        compiler_params=pltpu.CompilerParams(vmem_limit_bytes=16 * 2**20),
        cost_estimate=pl.CostEstimate(flops=51_000_000, bytes_accessed=3_000_000, transcendentals=0),
        name="momentum_and_weight",
    )(momentum, compressed.reshape(RANK, COLS), projection, weight.T)
    return (new_momentum, new_weight.T)


def solution(mesh):
    return jax.shard_map(
        shards,
        mesh=mesh,
        in_specs=(P("dp", "mp"), P("dp", "mp"), P("dp", None), P("mp", None), P("mp", "dp")),
        out_specs=(P("mp", None), P("mp", "dp")),
        check_vma=False,
    )
```

```python
import functools
import math

import jax
import jax.numpy as jnp
from jax import lax
from jax.experimental import pallas as pl
from jax.experimental.pallas import tpu as pltpu
from jax.sharding import PartitionSpec as P

MESH = pl.DeviceIdType.MESH
BF16 = jnp.bfloat16
F32 = jnp.float32

NZ, NM = 16, 8
BLK = 112
SL = 16
SLICES = 7
TOK, COLS, RANK = 256, 896, 256
HALF = RANK // 2
PIECE = TOK // NM
CHUNKS = HALF // SL
NEAR = (0, 1, -1, -2)
REACH = (4, 12, 3, 13, 2, 14, 1, 15)
PEERS = ((2, 1), (1, 1), (3, 1), (2, 0), (0, 1), (1, 0), (3, 0))
SCATTER = tuple((dy, mt) for dy in (1, 0) for mt in (0, 1, 2, 3, 4, 5, 6, None) if dy or mt is not None)


def kernel(
    factor,
    a_hbm, g_hbm, p_hbm,
    cres,
    a, g, p,
    gs, gq, pz, mine, part, rs, rsum, red,
    sb, rs2, far,
    in_sem,
    p1s, p1f, p1r, gss, gsr, xs, xr, a_s, a_r,
    r1s, r1r, r2s, r2r,
    d2s, d2r, d3s, d3r, d4s, d4r, d5s, d5r,
):
    dp, m = lax.axis_index("dp"), lax.axis_index("mp")
    z, yl, core = dp // 4, (dp // 2) % 2, dp % 2
    sign = 1 - 2 * core

    def dev(z_, yl_, core_, m_):
        return ((z_ * 2 + yl_) * 2 + core_, m_)

    sibling = dev(z, yl, 1 - core, m)

    def remote(src, dst, ssem, rsem, to):
        return pltpu.make_async_remote_copy(
            src_ref=src, dst_ref=dst, send_sem=ssem, recv_sem=rsem, device_id=to, device_id_type=MESH
        )

    def arrived(dst, rsem):
        remote(dst, dst, rsem, rsem, sibling).wait_recv()

    sent = []

    def send(src, dst, ssem, rsem, to):
        copy = remote(src, dst, ssem, rsem, to)
        copy.start()
        sent.append(copy)

    loads = [
        pltpu.make_async_copy(src, dst, in_sem.at[i])
        for i, (src, dst) in enumerate(((p_hbm, p), (g_hbm, g), (a_hbm, a.at[core])))
    ]
    for load in loads:
        load.start()

    peers = [((m // 2 + dx) % 4) * 2 + (m + dh) % 2 for dx, dh in PEERS]
    plane = [(mt, (yl + dy) % 2) for mt in peers for dy in (1, 0)] + [(m, 1 - yl)]

    barrier = pltpu.get_barrier_semaphore()

    def greet(to):
        pl.semaphore_signal(barrier, inc=1, device_id=to, device_id_type=MESH)

    for k in REACH:
        greet(dev((z + k) % NZ, yl, core, m))
    for mt, yt in plane:
        greet(dev(z, yt, core, mt))
    greet(sibling)
    loads[1].wait()
    for k in range(COLS // 128):
        tile = g[:, 128 * k : 128 * (k + 1)].T
        for i in range(128 // SL):
            group = k * (128 // SL) + i
            block, ms = group // SLICES, group % SLICES
            gs[(block // 2) % 2, ms, block % 2, block // 4] = tile[SL * i : SL * (i + 1)]

    loads[0].wait()
    pl.semaphore_wait(barrier, 8 + 15 + 1)

    slot = jnp.minimum(m, SLICES - 1)
    cut = pl.ds(pl.multiple_of(slot * SL, SL), SL)

    def along(k):
        return remote(p.at[cut], pz.at[core, z], p1s.at[k], p1r.at[z], dev((z + k) % NZ, yl, core, m))

    def onward(way, k):
        source = (z - 4 * way + NZ) % NZ
        return remote(
            pz.at[core, source], pz.at[core, source], p1f.at[way * sign + 1, k], p1r.at[source],
            dev((z + way * k + NZ) % NZ, yl, core, m),
        )

    def twin(source):
        return remote(pz.at[core, source], pz.at[core, source], xs.at[source], xr.at[source], sibling)

    ways = ((sign, (4, 3, 2, 1)), (-sign, (3, 2, 1)))

    @pl.when(m < SLICES)
    def _():
        for k in REACH[:2]:
            along(k).start()
        pz[core, z] = p[cut]
        twin(z).start()

    def spread(j):
        mt, yt = plane[j]
        mt = jnp.minimum(mt, SLICES - 1)
        return remote(gs.at[yt, mt], gq.at[yl, m], gss.at[j], gsr.at[yl, m], dev(z, yt, core, mt))

    for j, (mt, _) in enumerate(plane):
        @pl.when(mt < SLICES)
        def _():
            spread(j).start()

    loads[2].wait()
    send(a.at[core], a.at[core], a_s, a_r, sibling)

    @pl.when(m < SLICES)
    def _():
        gq[yl, m] = gs[yl, slot]
        for way, steps in ways:
            source = (z - 4 * way + NZ) % NZ
            arrived(pz.at[core, source], p1r.at[source])
            for k in steps:
                onward(way, k).start()
            twin(source).start()
        for k in REACH[2:]:
            along(k).start()


    def piece(i):
        return pl.ds(pl.multiple_of(i * PIECE, PIECE), PIECE)

    def scatter(j):
        yt, mt = SCATTER[j][0], SCATTER[j][1]
        yt = (yl + yt) % 2
        mt = m if mt is None else peers[mt]
        return remote(part.at[yt, piece(mt)], rs.at[yl, slot], r1s.at[j], r1r.at[yl, slot], dev(z, yt, core, mt))

    @pl.when(m < SLICES)
    def _():
        for k in (1, 15, 2, 14, 3, 13, 5, 11, 6, 10, 7, 9, 8):
            source = (z + k) % NZ
            arrived(pz.at[core, source], p1r.at[source])
            twin(source).start()
        for mt, yt in reversed(plane):
            arrived(gq.at[yt, mt], gsr.at[yt, mt])
        turned = pz[core].reshape(NZ * SL, RANK).T
        for yt in range(2):
            there = gq[yt, :, core].reshape(NZ * SL, TOK)
            mine[yt] = jnp.dot(turned, there, preferred_element_type=F32)
        for k in range(NZ):
            arrived(pz.at[1 - core, k], xr.at[k])
        turned = pz[1 - core].reshape(NZ * SL, RANK).T
        for dy in (1, 0):
            yt = (yl + dy) % 2
            there = gq[yt, :, 1 - core].reshape(NZ * SL, TOK)
            part[yt] = (mine[yt] + jnp.dot(turned, there, preferred_element_type=F32)).astype(BF16)
            for j, (step_y, _) in enumerate(SCATTER):
                if step_y == dy:
                    scatter(j).start()
        rs[yl, slot] = part[yl, piece(m)]

    for ms in range(SLICES):
        for ys in range(2):
            @pl.when((ms != m) | (ys != yl))
            def _():
                arrived(rs.at[ys, ms], r1r.at[ys, ms])

    total = rs[0, 0].astype(F32) + rs[1, 0].astype(F32)
    for ms in range(1, SLICES):
        total += rs[0, ms].astype(F32) + rs[1, ms].astype(F32)
    rsum[...] = total.astype(BF16)
    def to_owner(q, dy):
        delta = (q - z + NZ) % 4
        zo = (z + jnp.where(delta == 2, -2 * sign, jnp.where(delta == 3, -1, delta)) + NZ) % NZ
        i = jnp.where(delta == 0, 0, jnp.where(delta == 2, 3, jnp.where((delta == 1) == (core == 0), 1, 2)))
        yo = (yl + dy) % 2
        return remote(sb.at[2 * q + yo], rs2.at[i, yl], d2s.at[q, dy], d2r.at[i, yl], dev(zo, yo, core, m))

    arrived(a.at[1 - core], a_r)
    half = m // 4
    place = red.at[core, piece(m % 4)]
    for k, mt in enumerate(peers):
        send(rsum, place, r2s.at[k], r2r.at[core, m % 4], dev(z, yl, half, mt))

    def across():
        return remote(rsum, place, r2s.at[7], r2r.at[core, m % 4], sibling)

    @pl.when(half != core)
    def _():
        across().start()

    @pl.when(half == core)
    def _():
        red[core, piece(m % 4)] = rsum[...]

    x, h = m // 2, m % 2
    near_x = jnp.where((x - 2 * core + 4) % 4 < 2, (x - 2 * core + 4) % 4, jnp.where((x - 2 * core + 4) % 4 == 2, 1, 0))
    for dh, dx in ((0, 0), (0, 1), (1, 0), (1, 1)):
        q = ((near_x + dx) % 2) * 2 + (h + dh) % 2
        for c in range(2):
            @pl.when((c != core) | (4 * core + q != m))
            def _():
                arrived(red.at[c, piece(q)], r2r.at[c, q])

        total = jnp.dot(red[0, piece(q)], a[0], preferred_element_type=F32)
        total += jnp.dot(red[1, piece(q)], a[1], preferred_element_type=F32)
        sb[2 * q] = total[:SL].astype(BF16)
        sb[2 * q + 1] = total[SL:].astype(BF16)
        for dy in (1, 0):
            @pl.when((dy == 1) | (q != z % 4))
            def _():
                to_owner(q, dy).start()

    rs2[0, yl] = sb[2 * (z % 4) + yl]
    zh = z // 4
    arrived(rs2.at[0, 1 - yl], d2r.at[0, 1 - yl])
    for i in (1, 2, 3):
        for y in range(2):
            arrived(rs2.at[i, y], d2r.at[i, y])
    total = rs2[0, 0].astype(F32) + rs2[0, 1].astype(F32)
    for i in (1, 2, 3):
        total += rs2[i, 0].astype(F32) + rs2[i, 1].astype(F32)
    far[zh] = total.astype(BF16)
    send(far.at[zh], far.at[zh], d3s.at[2], d3r.at[zh], dev((z + 8) % NZ, yl, core, m))

    for j, (mt, _) in enumerate(plane):
        @pl.when(mt < SLICES)
        def _():
            spread(j).wait_send()

    @pl.when(half != core)
    def _():
        across().wait_send()

    @pl.when(m < SLICES)
    def _():
        for k in REACH:
            along(k).wait_send()
        for way, steps in ways:
            for k in steps:
                onward(way, k).wait_send()
        for k in range(NZ):
            twin(k).wait_send()
        for j in range(len(SCATTER)):
            scatter(j).wait_send()

    for copy in sent[:-1]:
        copy.wait_send()
    del sent[:-1]
    for q in range(4):
        for dy in (1, 0):
            @pl.when((dy == 1) | (q != z % 4))
            def _():
                to_owner(q, dy).wait_send()
    for k in (1, 3):
        send(far.at[zh], far.at[zh], d3s.at[k], d3r.at[zh], dev((z + 4 * k) % NZ, yl, core, m))
    for k in (1, 3, 2):
        arrived(far.at[(zh + k) % 4], d3r.at[(zh + k) % 4])
    total = far[0].astype(F32)
    for i in range(1, 4):
        total += far[i].astype(F32)
    own = 2 * (z % 4) + yl
    cres[core, own] = (total * factor).astype(BF16)
    place = cres.at[core, own]
    for i in (3, 1, 2, 0):
        zu = (z - sign * NEAR[i] + NZ) % NZ
        for dy in (1, 0):
            if i > 0 or dy == 1:
                send(place, place, d4s.at[i, dy], d4r.at[i, yl], dev(zu, (yl + dy) % 2, core, m))
    send(place, place, d5s.at[0, 0], d5r.at[0, 0], sibling)
    for i in (0, 1, 2, 3):
        zo = (z + sign * NEAR[i] + NZ) % NZ
        for dy in (0, 1):
            if i > 0 or dy == 1:
                yo = (yl + dy) % 2
                place = cres.at[core, 2 * (zo % 4) + yo]
                arrived(place, d4r.at[i, yo])
                send(place, place, d5s.at[i, dy], d5r.at[i, dy], sibling)
    for i in (0, 1, 2, 3):
        zo = (z - sign * NEAR[i] + NZ) % NZ
        for dy in (0, 1):
            arrived(cres.at[1 - core, 2 * (zo % 4) + (yl + dy) % 2], d5r.at[i, dy])

    for copy in sent:
        copy.wait_send()


def step(m_ref, c_ref, p_ref, w_ref, m_out, w_out, mom, wei, sem):
    copies = []

    def leave(src, dst, i):
        copies.append(pltpu.make_async_copy(src, dst, sem.at[i]))
        copies[-1].start()

    tiles = [slice(128 * k, 128 * (k + 1)) for k in range(COLS // 128)]
    for k, rows in enumerate(tiles):
        mom[rows] = 0.9 * m_ref[rows] + c_ref[:, rows].T.astype(F32)
        leave(mom.at[rows], m_out.at[rows], k)
    for k, rows in enumerate(tiles):
        update = lax.dot_general(
            p_ref[...], mom[rows].astype(BF16), (((1,), (1,)), ((), ())), preferred_element_type=F32
        )
        wei[:, rows] = (w_ref[:, rows].astype(F32) - 2.0 * update).astype(BF16)
        leave(wei.at[:, rows], w_out.at[:, rows], len(tiles) + k)
    for copy in copies:
        copy.wait()


def shards(attn_out, out_grad, projection, momentum, weight):
    factor = 1.0 / math.sqrt(attn_out.shape[0] * lax.axis_size("dp"))
    vmem, dma = pltpu.VMEM, pltpu.SemaphoreType.DMA
    compressed = pl.pallas_call(
        functools.partial(kernel, factor),
        out_shape=jax.ShapeDtypeStruct((2, CHUNKS, SL, COLS), BF16),
        in_specs=[pl.BlockSpec(memory_space=pltpu.HBM)] * 3,
        out_specs=pl.BlockSpec(memory_space=vmem),
        scratch_shapes=[
            vmem((2, TOK, COLS), BF16), vmem((TOK, COLS), BF16), vmem((BLK, RANK), BF16),
            vmem((2, SLICES, 2, 2, SL, TOK), BF16), vmem((2, NM, 2, 2, SL, TOK), BF16), vmem((2, NZ, SL, RANK), BF16),
            vmem((2, RANK, TOK), F32), vmem((2, RANK, TOK), BF16), vmem((2, SLICES, PIECE, TOK), BF16),
            vmem((PIECE, TOK), BF16), vmem((2, HALF, TOK), BF16),
            vmem((CHUNKS, SL, COLS), BF16), vmem((4, 2, SL, COLS), BF16), vmem((4, SL, COLS), BF16),
            dma((3,)),
            dma((NZ,)), dma((3, 5)), dma((NZ,)), dma((15,)), dma((2, NM)), dma((NZ,)), dma((NZ,)), dma, dma,
            dma((15,)), dma((2, SLICES)), dma((NM,)), dma((2, 4)),
            dma((4, 2)), dma((4, 2)), dma((4,)), dma((4,)),
            dma((4, 2)), dma((4, 2)), dma((4, 2)), dma((4, 2)),
        ],
        compiler_params=pltpu.CompilerParams(
            collective_id=0, has_side_effects=True, vmem_limit_bytes=32 * 2**20
        ),
        cost_estimate=pl.CostEstimate(flops=300_000_000, bytes_accessed=4_000_000, transcendentals=0),
        name="compress",
    )(*(pltpu.with_memory_space_constraint(x, pltpu.HBM) for x in (attn_out, out_grad, projection)))
    new_momentum, new_weight = pl.pallas_call(
        step,
        out_shape=(
            jax.ShapeDtypeStruct((COLS, RANK), F32),
            jax.ShapeDtypeStruct((BLK, COLS), BF16),
        ),
        in_specs=[pl.BlockSpec(memory_space=vmem)] * 4,
        out_specs=(pl.BlockSpec(memory_space=pltpu.HBM), pl.BlockSpec(memory_space=pltpu.HBM)),
        scratch_shapes=[vmem((COLS, RANK), F32), vmem((BLK, COLS), BF16), dma((2 * COLS // 128,))],
        compiler_params=pltpu.CompilerParams(vmem_limit_bytes=16 * 2**20),
        cost_estimate=pl.CostEstimate(flops=51_000_000, bytes_accessed=3_000_000, transcendentals=0),
        name="momentum_and_weight",
    )(momentum, compressed.reshape(RANK, COLS), projection, weight.T)
    return (new_momentum, new_weight.T)


def solution(mesh):
    return jax.shard_map(
        shards,
        mesh=mesh,
        in_specs=(P("dp", "mp"), P("dp", "mp"), P("dp", None), P("mp", None), P("mp", "dp")),
        out_specs=(P("mp", None), P("mp", "dp")),
        check_vma=False,
    )
```

```python
import functools
import math

import jax
import jax.numpy as jnp
from jax import lax
from jax.experimental import pallas as pl
from jax.experimental.pallas import tpu as pltpu
from jax.sharding import PartitionSpec as P

MESH = pl.DeviceIdType.MESH
BF16 = jnp.bfloat16
F32 = jnp.float32

NZ, NM = 16, 8
BLK = 112
SL = 16
SLICES = 7
TOK, COLS, RANK = 256, 896, 256
HALF = RANK // 2
PIECE = TOK // NM
PARTS = (slice(0, 512), slice(512, COLS))
CHUNKS = HALF // SL
NEAR = (0, 1, -1, -2)
REACH = (4, 12, 3, 13, 2, 14, 1, 15)
PEERS = ((2, 1), (1, 1), (3, 1), (2, 0), (0, 1), (1, 0), (3, 0))
SCATTER = tuple((dy, mt) for dy in (1, 0) for mt in (0, 1, 2, 3, 4, 5, 6, None) if dy or mt is not None)


def kernel(
    factor,
    a_hbm, g_hbm, p_hbm,
    cres,
    a, g, p,
    gs, gq, pz, mine, part, rs, rsum, red,
    sb, rs2, far,
    in_sem,
    p1s, p1f, p1r, gss, gsr, xs, xr, a_s, a_r,
    r1s, r1r, r2s, r2r,
    d2s, d2r, d3s, d3r, d4s, d4r, d5s, d5r,
):
    dp, m = lax.axis_index("dp"), lax.axis_index("mp")
    z, yl, core = dp // 4, (dp // 2) % 2, dp % 2
    sign = 1 - 2 * core

    def dev(z_, yl_, core_, m_):
        return ((z_ * 2 + yl_) * 2 + core_, m_)

    sibling = dev(z, yl, 1 - core, m)

    def remote(src, dst, ssem, rsem, to):
        return pltpu.make_async_remote_copy(
            src_ref=src, dst_ref=dst, send_sem=ssem, recv_sem=rsem, device_id=to, device_id_type=MESH
        )

    def arrived(dst, rsem):
        remote(dst, dst, rsem, rsem, sibling).wait_recv()

    sent = []

    def send(src, dst, ssem, rsem, to):
        copy = remote(src, dst, ssem, rsem, to)
        copy.start()
        sent.append(copy)

    loads = [
        pltpu.make_async_copy(src, dst, in_sem.at[i])
        for i, (src, dst) in enumerate(((p_hbm, p), (g_hbm, g), (a_hbm, a.at[core])))
    ]
    for load in loads:
        load.start()

    peers = [((m // 2 + dx) % 4) * 2 + (m + dh) % 2 for dx, dh in PEERS]
    plane = [(mt, (yl + dy) % 2) for mt in peers for dy in (1, 0)] + [(m, 1 - yl)]

    barrier = pltpu.get_barrier_semaphore()

    def greet(to):
        pl.semaphore_signal(barrier, inc=1, device_id=to, device_id_type=MESH)

    for k in REACH:
        greet(dev((z + k) % NZ, yl, core, m))
    for mt, yt in plane:
        greet(dev(z, yt, core, mt))
    greet(sibling)
    loads[1].wait()
    for k in range(COLS // 128):
        tile = g[:, 128 * k : 128 * (k + 1)].T
        for i in range(128 // SL):
            group = k * (128 // SL) + i
            block, ms = group // SLICES, group % SLICES
            gs[(block // 2) % 2, ms, block % 2, block // 4] = tile[SL * i : SL * (i + 1)]

    loads[0].wait()
    pl.semaphore_wait(barrier, 8 + 15 + 1)

    slot = jnp.minimum(m, SLICES - 1)
    cut = pl.ds(pl.multiple_of(slot * SL, SL), SL)

    def along(k):
        return remote(p.at[cut], pz.at[core, z], p1s.at[k], p1r.at[z], dev((z + k) % NZ, yl, core, m))

    def onward(way, k):
        source = (z - 4 * way + NZ) % NZ
        return remote(
            pz.at[core, source], pz.at[core, source], p1f.at[way * sign + 1, k], p1r.at[source],
            dev((z + way * k + NZ) % NZ, yl, core, m),
        )

    def twin(source):
        return remote(pz.at[core, source], pz.at[core, source], xs.at[source], xr.at[source], sibling)

    ways = ((sign, (4, 3, 2, 1)), (-sign, (3, 2, 1)))

    @pl.when(m < SLICES)
    def _():
        for k in REACH:
            along(k).start()
        pz[core, z] = p[cut]
        twin(z).start()

    def spread(j):
        mt, yt = plane[j]
        mt = jnp.minimum(mt, SLICES - 1)
        return remote(gs.at[yt, mt], gq.at[yl, m], gss.at[j], gsr.at[yl, m], dev(z, yt, core, mt))

    for j, (mt, _) in enumerate(plane):
        @pl.when(mt < SLICES)
        def _():
            spread(j).start()

    loads[2].wait()
    send(a.at[core], a.at[core], a_s, a_r, sibling)

    @pl.when(m < SLICES)
    def _():
        gq[yl, m] = gs[yl, slot]
        for way, steps in ways:
            source = (z - 4 * way + NZ) % NZ
            arrived(pz.at[core, source], p1r.at[source])
            for k in steps:
                onward(way, k).start()
            twin(source).start()


    def piece(i):
        return pl.ds(pl.multiple_of(i * PIECE, PIECE), PIECE)

    def scatter(j):
        yt, mt = SCATTER[j][0], SCATTER[j][1]
        yt = (yl + yt) % 2
        mt = m if mt is None else peers[mt]
        return remote(part.at[yt, piece(mt)], rs.at[yl, slot], r1s.at[j], r1r.at[yl, slot], dev(z, yt, core, mt))

    @pl.when(m < SLICES)
    def _():
        for k in (1, 15, 2, 14, 3, 13, 5, 11, 6, 10, 7, 9, 8):
            source = (z + k) % NZ
            arrived(pz.at[core, source], p1r.at[source])
            twin(source).start()
        for mt, yt in reversed(plane):
            arrived(gq.at[yt, mt], gsr.at[yt, mt])
        turned = pz[core].reshape(NZ * SL, RANK).T
        for yt in range(2):
            there = gq[yt, :, core].reshape(NZ * SL, TOK)
            mine[yt] = jnp.dot(turned, there, preferred_element_type=F32)
        for k in range(NZ):
            arrived(pz.at[1 - core, k], xr.at[k])
        turned = pz[1 - core].reshape(NZ * SL, RANK).T
        for dy in (1, 0):
            yt = (yl + dy) % 2
            there = gq[yt, :, 1 - core].reshape(NZ * SL, TOK)
            part[yt] = (mine[yt] + jnp.dot(turned, there, preferred_element_type=F32)).astype(BF16)
            for j, (step_y, _) in enumerate(SCATTER):
                if step_y == dy:
                    scatter(j).start()
        rs[yl, slot] = part[yl, piece(m)]

    for ms in range(SLICES):
        for ys in range(2):
            @pl.when((ms != m) | (ys != yl))
            def _():
                arrived(rs.at[ys, ms], r1r.at[ys, ms])

    total = rs[0, 0].astype(F32) + rs[1, 0].astype(F32)
    for ms in range(1, SLICES):
        total += rs[0, ms].astype(F32) + rs[1, ms].astype(F32)
    rsum[...] = total.astype(BF16)
    def to_owner(q, dy):
        delta = (q - z + NZ) % 4
        zo = (z + jnp.where(delta == 2, -2 * sign, jnp.where(delta == 3, -1, delta)) + NZ) % NZ
        i = jnp.where(delta == 0, 0, jnp.where(delta == 2, 3, jnp.where((delta == 1) == (core == 0), 1, 2)))
        yo = (yl + dy) % 2
        return remote(sb.at[2 * q + yo], rs2.at[i, yl], d2s.at[q, dy], d2r.at[i, yl], dev(zo, yo, core, m))

    arrived(a.at[1 - core], a_r)
    half = m // 4
    place = red.at[core, piece(m % 4)]
    for k, mt in enumerate(peers):
        send(rsum, place, r2s.at[k], r2r.at[core, m % 4], dev(z, yl, half, mt))

    def across():
        return remote(rsum, place, r2s.at[7], r2r.at[core, m % 4], sibling)

    @pl.when(half != core)
    def _():
        across().start()

    @pl.when(half == core)
    def _():
        red[core, piece(m % 4)] = rsum[...]

    x, h = m // 2, m % 2
    near_x = jnp.where((x - 2 * core + 4) % 4 < 2, (x - 2 * core + 4) % 4, jnp.where((x - 2 * core + 4) % 4 == 2, 1, 0))
    for dh, dx in ((0, 0), (0, 1), (1, 0), (1, 1)):
        q = ((near_x + dx) % 2) * 2 + (h + dh) % 2
        for c in range(2):
            @pl.when((c != core) | (4 * core + q != m))
            def _():
                arrived(red.at[c, piece(q)], r2r.at[c, q])

        total = jnp.dot(red[0, piece(q)], a[0], preferred_element_type=F32)
        total += jnp.dot(red[1, piece(q)], a[1], preferred_element_type=F32)
        sb[2 * q] = total[:SL].astype(BF16)
        sb[2 * q + 1] = total[SL:].astype(BF16)
        for dy in (1, 0):
            @pl.when((dy == 1) | (q != z % 4))
            def _():
                to_owner(q, dy).start()

    rs2[0, yl] = sb[2 * (z % 4) + yl]
    zh = z // 4
    arrived(rs2.at[0, 1 - yl], d2r.at[0, 1 - yl])
    for i in (1, 2, 3):
        for y in range(2):
            arrived(rs2.at[i, y], d2r.at[i, y])
    total = rs2[0, 0].astype(F32) + rs2[0, 1].astype(F32)
    for i in (1, 2, 3):
        total += rs2[i, 0].astype(F32) + rs2[i, 1].astype(F32)
    far[zh] = total.astype(BF16)
    for b, lanes in enumerate(PARTS):
        for k in (2, 1, 3):
            place = far.at[zh, :, lanes]
            send(place, place, d3s.at[b, k], d3r.at[b, zh], dev((z + 4 * k) % NZ, yl, core, m))

    for j, (mt, _) in enumerate(plane):
        @pl.when(mt < SLICES)
        def _():
            spread(j).wait_send()

    @pl.when(half != core)
    def _():
        across().wait_send()

    @pl.when(m < SLICES)
    def _():
        for k in REACH:
            along(k).wait_send()
        for way, steps in ways:
            for k in steps:
                onward(way, k).wait_send()
        for k in range(NZ):
            twin(k).wait_send()
        for j in range(len(SCATTER)):
            scatter(j).wait_send()

    for copy in sent[:-6]:
        copy.wait_send()
    del sent[:-6]
    for q in range(4):
        for dy in (1, 0):
            @pl.when((dy == 1) | (q != z % 4))
            def _():
                to_owner(q, dy).wait_send()
    own = 2 * (z % 4) + yl
    for b, lanes in enumerate(PARTS):
        for k in (1, 3, 2):
            arrived(far.at[(zh + k) % 4, :, lanes], d3r.at[b, (zh + k) % 4])
        total = far[0, :, lanes].astype(F32)
        for i in range(1, 4):
            total += far[i, :, lanes].astype(F32)
        cres[core, own, :, lanes] = (total * factor).astype(BF16)
        place = cres.at[core, own, :, lanes]
        for i in (3, 1, 2, 0):
            zu = (z - sign * NEAR[i] + NZ) % NZ
            for dy in (1, 0):
                if i > 0 or dy == 1:
                    send(place, place, d4s.at[b, i, dy], d4r.at[b, i, yl], dev(zu, (yl + dy) % 2, core, m))
        send(place, place, d5s.at[b, 0, 0], d5r.at[b, 0, 0], sibling)
    for b, lanes in enumerate(PARTS):
        for i in (0, 1, 2, 3):
            zo = (z + sign * NEAR[i] + NZ) % NZ
            for dy in (0, 1):
                if i > 0 or dy == 1:
                    yo = (yl + dy) % 2
                    place = cres.at[core, 2 * (zo % 4) + yo, :, lanes]
                    arrived(place, d4r.at[b, i, yo])
                    send(place, place, d5s.at[b, i, dy], d5r.at[b, i, dy], sibling)
    for b, lanes in enumerate(PARTS):
        for i in (0, 1, 2, 3):
            zo = (z - sign * NEAR[i] + NZ) % NZ
            for dy in (0, 1):
                arrived(cres.at[1 - core, 2 * (zo % 4) + (yl + dy) % 2, :, lanes], d5r.at[b, i, dy])

    for copy in sent:
        copy.wait_send()


def step(m_ref, c_ref, p_ref, w_ref, m_out, w_out, mom, wei, sem):
    copies = []

    def leave(src, dst, i):
        copies.append(pltpu.make_async_copy(src, dst, sem.at[i]))
        copies[-1].start()

    tiles = [slice(128 * k, 128 * (k + 1)) for k in range(COLS // 128)]
    for k, rows in enumerate(tiles):
        mom[rows] = 0.9 * m_ref[rows] + c_ref[:, rows].T.astype(F32)
        leave(mom.at[rows], m_out.at[rows], k)
    for k, rows in enumerate(tiles):
        update = lax.dot_general(
            p_ref[...], mom[rows].astype(BF16), (((1,), (1,)), ((), ())), preferred_element_type=F32
        )
        wei[:, rows] = (w_ref[:, rows].astype(F32) - 2.0 * update).astype(BF16)
        leave(wei.at[:, rows], w_out.at[:, rows], len(tiles) + k)
    for copy in copies:
        copy.wait()


def shards(attn_out, out_grad, projection, momentum, weight):
    factor = 1.0 / math.sqrt(attn_out.shape[0] * lax.axis_size("dp"))
    vmem, dma = pltpu.VMEM, pltpu.SemaphoreType.DMA
    compressed = pl.pallas_call(
        functools.partial(kernel, factor),
        out_shape=jax.ShapeDtypeStruct((2, CHUNKS, SL, COLS), BF16),
        in_specs=[pl.BlockSpec(memory_space=pltpu.HBM)] * 3,
        out_specs=pl.BlockSpec(memory_space=vmem),
        scratch_shapes=[
            vmem((2, TOK, COLS), BF16), vmem((TOK, COLS), BF16), vmem((BLK, RANK), BF16),
            vmem((2, SLICES, 2, 2, SL, TOK), BF16), vmem((2, NM, 2, 2, SL, TOK), BF16), vmem((2, NZ, SL, RANK), BF16),
            vmem((2, RANK, TOK), F32), vmem((2, RANK, TOK), BF16), vmem((2, SLICES, PIECE, TOK), BF16),
            vmem((PIECE, TOK), BF16), vmem((2, HALF, TOK), BF16),
            vmem((CHUNKS, SL, COLS), BF16), vmem((4, 2, SL, COLS), BF16), vmem((4, SL, COLS), BF16),
            dma((3,)),
            dma((NZ,)), dma((3, 5)), dma((NZ,)), dma((15,)), dma((2, NM)), dma((NZ,)), dma((NZ,)), dma, dma,
            dma((15,)), dma((2, SLICES)), dma((NM,)), dma((2, 4)),
            dma((4, 2)), dma((4, 2)), dma((2, 4)), dma((2, 4)),
            dma((2, 4, 2)), dma((2, 4, 2)), dma((2, 4, 2)), dma((2, 4, 2)),
        ],
        compiler_params=pltpu.CompilerParams(
            collective_id=0, has_side_effects=True, vmem_limit_bytes=32 * 2**20
        ),
        cost_estimate=pl.CostEstimate(flops=300_000_000, bytes_accessed=4_000_000, transcendentals=0),
        name="compress",
    )(*(pltpu.with_memory_space_constraint(x, pltpu.HBM) for x in (attn_out, out_grad, projection)))
    new_momentum, new_weight = pl.pallas_call(
        step,
        out_shape=(
            jax.ShapeDtypeStruct((COLS, RANK), F32),
            jax.ShapeDtypeStruct((BLK, COLS), BF16),
        ),
        in_specs=[pl.BlockSpec(memory_space=vmem)] * 4,
        out_specs=(pl.BlockSpec(memory_space=pltpu.HBM), pl.BlockSpec(memory_space=pltpu.HBM)),
        scratch_shapes=[vmem((COLS, RANK), F32), vmem((BLK, COLS), BF16), dma((2 * COLS // 128,))],
        compiler_params=pltpu.CompilerParams(vmem_limit_bytes=16 * 2**20),
        cost_estimate=pl.CostEstimate(flops=51_000_000, bytes_accessed=3_000_000, transcendentals=0),
        name="momentum_and_weight",
    )(momentum, compressed.reshape(RANK, COLS), projection, weight.T)
    return (new_momentum, new_weight.T)


def solution(mesh):
    return jax.shard_map(
        shards,
        mesh=mesh,
        in_specs=(P("dp", "mp"), P("dp", "mp"), P("dp", None), P("mp", None), P("mp", "dp")),
        out_specs=(P("mp", None), P("mp", "dp")),
        check_vma=False,
    )
```

```python
import functools
import math

import jax
import jax.numpy as jnp
from jax import lax
from jax.experimental import pallas as pl
from jax.experimental.pallas import tpu as pltpu
from jax.sharding import PartitionSpec as P

MESH = pl.DeviceIdType.MESH
BF16 = jnp.bfloat16
F32 = jnp.float32

NZ, NM = 16, 8
BLK = 112
SL = 16
SLICES = 7
TOK, COLS, RANK = 256, 896, 256
HALF = RANK // 2
PIECE = TOK // NM
PARTS = (slice(0, 384), slice(384, 640), slice(640, COLS))
CHUNKS = HALF // SL
NEAR = (0, 1, -1, -2)
REACH = (4, 12, 3, 13, 2, 14, 1, 15)
PEERS = ((2, 1), (1, 1), (3, 1), (2, 0), (0, 1), (1, 0), (3, 0))
SCATTER = tuple((dy, mt) for dy in (1, 0) for mt in (0, 1, 2, 3, 4, 5, 6, None) if dy or mt is not None)


def kernel(
    factor,
    a_hbm, g_hbm, p_hbm,
    cres,
    a, g, p,
    gs, gq, pz, mine, part, rs, rsum, red,
    sb, rs2, far,
    in_sem,
    p1s, p1f, p1r, gss, gsr, xs, xr, a_s, a_r,
    r1s, r1r, r2s, r2r,
    d2s, d2r, d3s, d3r, d4s, d4r, d5s, d5r,
):
    dp, m = lax.axis_index("dp"), lax.axis_index("mp")
    z, yl, core = dp // 4, (dp // 2) % 2, dp % 2
    sign = 1 - 2 * core

    def dev(z_, yl_, core_, m_):
        return ((z_ * 2 + yl_) * 2 + core_, m_)

    sibling = dev(z, yl, 1 - core, m)

    def remote(src, dst, ssem, rsem, to):
        return pltpu.make_async_remote_copy(
            src_ref=src, dst_ref=dst, send_sem=ssem, recv_sem=rsem, device_id=to, device_id_type=MESH
        )

    def arrived(dst, rsem):
        remote(dst, dst, rsem, rsem, sibling).wait_recv()

    sent = []

    def send(src, dst, ssem, rsem, to):
        copy = remote(src, dst, ssem, rsem, to)
        copy.start()
        sent.append(copy)

    loads = [
        pltpu.make_async_copy(src, dst, in_sem.at[i])
        for i, (src, dst) in enumerate(((p_hbm, p), (g_hbm, g), (a_hbm, a.at[core])))
    ]
    for load in loads:
        load.start()

    peers = [((m // 2 + dx) % 4) * 2 + (m + dh) % 2 for dx, dh in PEERS]
    plane = [(mt, (yl + dy) % 2) for mt in peers for dy in (1, 0)] + [(m, 1 - yl)]

    barrier = pltpu.get_barrier_semaphore()

    def greet(to):
        pl.semaphore_signal(barrier, inc=1, device_id=to, device_id_type=MESH)

    for k in REACH:
        greet(dev((z + k) % NZ, yl, core, m))
    for mt, yt in plane:
        greet(dev(z, yt, core, mt))
    greet(sibling)
    loads[1].wait()
    for k in range(COLS // 128):
        tile = g[:, 128 * k : 128 * (k + 1)].T
        for i in range(128 // SL):
            group = k * (128 // SL) + i
            block, ms = group // SLICES, group % SLICES
            gs[(block // 2) % 2, ms, block % 2, block // 4] = tile[SL * i : SL * (i + 1)]

    loads[0].wait()
    pl.semaphore_wait(barrier, 8 + 15 + 1)

    slot = jnp.minimum(m, SLICES - 1)
    cut = pl.ds(pl.multiple_of(slot * SL, SL), SL)

    def along(k):
        return remote(p.at[cut], pz.at[core, z], p1s.at[k], p1r.at[z], dev((z + k) % NZ, yl, core, m))

    def onward(way, k):
        source = (z - 4 * way + NZ) % NZ
        return remote(
            pz.at[core, source], pz.at[core, source], p1f.at[way * sign + 1, k], p1r.at[source],
            dev((z + way * k + NZ) % NZ, yl, core, m),
        )

    def twin(source):
        return remote(pz.at[core, source], pz.at[core, source], xs.at[source], xr.at[source], sibling)

    ways = ((sign, (4, 3, 2, 1)), (-sign, (3, 2, 1)))

    @pl.when(m < SLICES)
    def _():
        for k in REACH:
            along(k).start()
        pz[core, z] = p[cut]
        twin(z).start()

    def spread(j):
        mt, yt = plane[j]
        mt = jnp.minimum(mt, SLICES - 1)
        return remote(gs.at[yt, mt], gq.at[yl, m], gss.at[j], gsr.at[yl, m], dev(z, yt, core, mt))

    for j, (mt, _) in enumerate(plane):
        @pl.when(mt < SLICES)
        def _():
            spread(j).start()

    loads[2].wait()
    send(a.at[core], a.at[core], a_s, a_r, sibling)

    @pl.when(m < SLICES)
    def _():
        gq[yl, m] = gs[yl, slot]
        for way, steps in ways:
            source = (z - 4 * way + NZ) % NZ
            arrived(pz.at[core, source], p1r.at[source])
            for k in steps:
                onward(way, k).start()
            twin(source).start()


    def piece(i):
        return pl.ds(pl.multiple_of(i * PIECE, PIECE), PIECE)

    def scatter(j):
        yt, mt = SCATTER[j][0], SCATTER[j][1]
        yt = (yl + yt) % 2
        mt = m if mt is None else peers[mt]
        return remote(part.at[yt, piece(mt)], rs.at[yl, slot], r1s.at[j], r1r.at[yl, slot], dev(z, yt, core, mt))

    @pl.when(m < SLICES)
    def _():
        for k in (1, 15, 2, 14, 3, 13, 5, 11, 6, 10, 7, 9, 8):
            source = (z + k) % NZ
            arrived(pz.at[core, source], p1r.at[source])
            twin(source).start()
        for mt, yt in reversed(plane):
            arrived(gq.at[yt, mt], gsr.at[yt, mt])
        turned = pz[core].reshape(NZ * SL, RANK).T
        for yt in range(2):
            there = gq[yt, :, core].reshape(NZ * SL, TOK)
            mine[yt] = jnp.dot(turned, there, preferred_element_type=F32)
        for k in range(NZ):
            arrived(pz.at[1 - core, k], xr.at[k])
        turned = pz[1 - core].reshape(NZ * SL, RANK).T
        for dy in (1, 0):
            yt = (yl + dy) % 2
            there = gq[yt, :, 1 - core].reshape(NZ * SL, TOK)
            part[yt] = (mine[yt] + jnp.dot(turned, there, preferred_element_type=F32)).astype(BF16)
            for j, (step_y, _) in enumerate(SCATTER):
                if step_y == dy:
                    scatter(j).start()
        rs[yl, slot] = part[yl, piece(m)]

    for ms in range(SLICES):
        for ys in range(2):
            @pl.when((ms != m) | (ys != yl))
            def _():
                arrived(rs.at[ys, ms], r1r.at[ys, ms])

    total = rs[0, 0].astype(F32) + rs[1, 0].astype(F32)
    for ms in range(1, SLICES):
        total += rs[0, ms].astype(F32) + rs[1, ms].astype(F32)
    rsum[...] = total.astype(BF16)
    def to_owner(q, dy):
        delta = (q - z + NZ) % 4
        zo = (z + jnp.where(delta == 2, -2 * sign, jnp.where(delta == 3, -1, delta)) + NZ) % NZ
        i = jnp.where(delta == 0, 0, jnp.where(delta == 2, 3, jnp.where((delta == 1) == (core == 0), 1, 2)))
        yo = (yl + dy) % 2
        return remote(sb.at[2 * q + yo], rs2.at[i, yl], d2s.at[q, dy], d2r.at[i, yl], dev(zo, yo, core, m))

    arrived(a.at[1 - core], a_r)
    half = m // 4
    place = red.at[core, piece(m % 4)]
    for k, mt in enumerate(peers):
        send(rsum, place, r2s.at[k], r2r.at[core, m % 4], dev(z, yl, half, mt))

    def across():
        return remote(rsum, place, r2s.at[7], r2r.at[core, m % 4], sibling)

    @pl.when(half != core)
    def _():
        across().start()

    @pl.when(half == core)
    def _():
        red[core, piece(m % 4)] = rsum[...]

    x, h = m // 2, m % 2
    near_x = jnp.where((x - 2 * core + 4) % 4 < 2, (x - 2 * core + 4) % 4, jnp.where((x - 2 * core + 4) % 4 == 2, 1, 0))
    for dh, dx in ((0, 0), (0, 1), (1, 0), (1, 1)):
        q = ((near_x + dx) % 2) * 2 + (h + dh) % 2
        for c in range(2):
            @pl.when((c != core) | (4 * core + q != m))
            def _():
                arrived(red.at[c, piece(q)], r2r.at[c, q])

        total = jnp.dot(red[0, piece(q)], a[0], preferred_element_type=F32)
        total += jnp.dot(red[1, piece(q)], a[1], preferred_element_type=F32)
        sb[2 * q] = total[:SL].astype(BF16)
        sb[2 * q + 1] = total[SL:].astype(BF16)
        for dy in (1, 0):
            @pl.when((dy == 1) | (q != z % 4))
            def _():
                to_owner(q, dy).start()

    rs2[0, yl] = sb[2 * (z % 4) + yl]
    zh = z // 4
    arrived(rs2.at[0, 1 - yl], d2r.at[0, 1 - yl])
    for i in (1, 2, 3):
        for y in range(2):
            arrived(rs2.at[i, y], d2r.at[i, y])
    total = rs2[0, 0].astype(F32) + rs2[0, 1].astype(F32)
    for i in (1, 2, 3):
        total += rs2[i, 0].astype(F32) + rs2[i, 1].astype(F32)
    far[zh] = total.astype(BF16)
    for b, lanes in enumerate(PARTS):
        for k in (2, 1, 3):
            place = far.at[zh, :, lanes]
            send(place, place, d3s.at[b, k], d3r.at[b, zh], dev((z + 4 * k) % NZ, yl, core, m))

    for j, (mt, _) in enumerate(plane):
        @pl.when(mt < SLICES)
        def _():
            spread(j).wait_send()

    @pl.when(half != core)
    def _():
        across().wait_send()

    @pl.when(m < SLICES)
    def _():
        for k in REACH:
            along(k).wait_send()
        for way, steps in ways:
            for k in steps:
                onward(way, k).wait_send()
        for k in range(NZ):
            twin(k).wait_send()
        for j in range(len(SCATTER)):
            scatter(j).wait_send()

    for copy in sent[:-9]:
        copy.wait_send()
    del sent[:-9]
    for q in range(4):
        for dy in (1, 0):
            @pl.when((dy == 1) | (q != z % 4))
            def _():
                to_owner(q, dy).wait_send()
    own = 2 * (z % 4) + yl
    for b, lanes in enumerate(PARTS):
        for k in (1, 3, 2):
            arrived(far.at[(zh + k) % 4, :, lanes], d3r.at[b, (zh + k) % 4])
        total = far[0, :, lanes].astype(F32)
        for i in range(1, 4):
            total += far[i, :, lanes].astype(F32)
        cres[core, own, :, lanes] = (total * factor).astype(BF16)
        place = cres.at[core, own, :, lanes]
        for i in (3, 1, 2, 0):
            zu = (z - sign * NEAR[i] + NZ) % NZ
            for dy in (1, 0):
                if i > 0 or dy == 1:
                    send(place, place, d4s.at[b, i, dy], d4r.at[b, i, yl], dev(zu, (yl + dy) % 2, core, m))
        send(place, place, d5s.at[b, 0, 0], d5r.at[b, 0, 0], sibling)
    for b, lanes in enumerate(PARTS):
        for i in (0, 1, 2, 3):
            zo = (z + sign * NEAR[i] + NZ) % NZ
            for dy in (0, 1):
                if i > 0 or dy == 1:
                    yo = (yl + dy) % 2
                    place = cres.at[core, 2 * (zo % 4) + yo, :, lanes]
                    arrived(place, d4r.at[b, i, yo])
                    send(place, place, d5s.at[b, i, dy], d5r.at[b, i, dy], sibling)
    for b, lanes in enumerate(PARTS):
        for i in (0, 1, 2, 3):
            zo = (z - sign * NEAR[i] + NZ) % NZ
            for dy in (0, 1):
                arrived(cres.at[1 - core, 2 * (zo % 4) + (yl + dy) % 2, :, lanes], d5r.at[b, i, dy])

    for copy in sent:
        copy.wait_send()


def step(m_ref, c_ref, p_ref, w_ref, m_out, w_out, mom, wei, sem):
    copies = []

    def leave(src, dst, i):
        copies.append(pltpu.make_async_copy(src, dst, sem.at[i]))
        copies[-1].start()

    tiles = [slice(128 * k, 128 * (k + 1)) for k in range(COLS // 128)]
    for k, rows in enumerate(tiles):
        mom[rows] = 0.9 * m_ref[rows] + c_ref[:, rows].T.astype(F32)
        leave(mom.at[rows], m_out.at[rows], k)
    for k, rows in enumerate(tiles):
        update = lax.dot_general(
            p_ref[...], mom[rows].astype(BF16), (((1,), (1,)), ((), ())), preferred_element_type=F32
        )
        wei[:, rows] = (w_ref[:, rows].astype(F32) - 2.0 * update).astype(BF16)
        leave(wei.at[:, rows], w_out.at[:, rows], len(tiles) + k)
    for copy in copies:
        copy.wait()


def shards(attn_out, out_grad, projection, momentum, weight):
    factor = 1.0 / math.sqrt(attn_out.shape[0] * lax.axis_size("dp"))
    vmem, dma = pltpu.VMEM, pltpu.SemaphoreType.DMA
    compressed = pl.pallas_call(
        functools.partial(kernel, factor),
        out_shape=jax.ShapeDtypeStruct((2, CHUNKS, SL, COLS), BF16),
        in_specs=[pl.BlockSpec(memory_space=pltpu.HBM)] * 3,
        out_specs=pl.BlockSpec(memory_space=vmem),
        scratch_shapes=[
            vmem((2, TOK, COLS), BF16), vmem((TOK, COLS), BF16), vmem((BLK, RANK), BF16),
            vmem((2, SLICES, 2, 2, SL, TOK), BF16), vmem((2, NM, 2, 2, SL, TOK), BF16), vmem((2, NZ, SL, RANK), BF16),
            vmem((2, RANK, TOK), F32), vmem((2, RANK, TOK), BF16), vmem((2, SLICES, PIECE, TOK), BF16),
            vmem((PIECE, TOK), BF16), vmem((2, HALF, TOK), BF16),
            vmem((CHUNKS, SL, COLS), BF16), vmem((4, 2, SL, COLS), BF16), vmem((4, SL, COLS), BF16),
            dma((3,)),
            dma((NZ,)), dma((3, 5)), dma((NZ,)), dma((15,)), dma((2, NM)), dma((NZ,)), dma((NZ,)), dma, dma,
            dma((15,)), dma((2, SLICES)), dma((NM,)), dma((2, 4)),
            dma((4, 2)), dma((4, 2)), dma((3, 4)), dma((3, 4)),
            dma((3, 4, 2)), dma((3, 4, 2)), dma((3, 4, 2)), dma((3, 4, 2)),
        ],
        compiler_params=pltpu.CompilerParams(
            collective_id=0, has_side_effects=True, vmem_limit_bytes=32 * 2**20
        ),
        cost_estimate=pl.CostEstimate(flops=300_000_000, bytes_accessed=4_000_000, transcendentals=0),
        name="compress",
    )(*(pltpu.with_memory_space_constraint(x, pltpu.HBM) for x in (attn_out, out_grad, projection)))
    new_momentum, new_weight = pl.pallas_call(
        step,
        out_shape=(
            jax.ShapeDtypeStruct((COLS, RANK), F32),
            jax.ShapeDtypeStruct((BLK, COLS), BF16),
        ),
        in_specs=[pl.BlockSpec(memory_space=vmem)] * 4,
        out_specs=(pl.BlockSpec(memory_space=pltpu.HBM), pl.BlockSpec(memory_space=pltpu.HBM)),
        scratch_shapes=[vmem((COLS, RANK), F32), vmem((BLK, COLS), BF16), dma((2 * COLS // 128,))],
        compiler_params=pltpu.CompilerParams(vmem_limit_bytes=16 * 2**20),
        cost_estimate=pl.CostEstimate(flops=51_000_000, bytes_accessed=3_000_000, transcendentals=0),
        name="momentum_and_weight",
    )(momentum, compressed.reshape(RANK, COLS), projection, weight.T)
    return (new_momentum, new_weight.T)


def solution(mesh):
    return jax.shard_map(
        shards,
        mesh=mesh,
        in_specs=(P("dp", "mp"), P("dp", "mp"), P("dp", None), P("mp", None), P("mp", "dp")),
        out_specs=(P("mp", None), P("mp", "dp")),
        check_vma=False,
    )
```
